128 devices in a mesh: enc: 4 (over x_hi, core), dp: 32 (over x_lo, z, y).
Axes of the slice: x: 4 (x_hi: 2, x_lo: 2; x = x_hi * 2 + x_lo), y: 4, z: 4, core: 2. Of those that a mesh axis runs over, the one named last changes fastest.
Arguments:
- sig_in: bfloat16 [12288, 1152], P('dp'), may hold values from -6 to 6
- sig_gain: float32 [1152], replicated, may hold values from 0.1 to 1.9
- sig_up: bfloat16 [1152, 4304], P(None, 'enc'), may hold values from -0.1875 to 0.1875
- sig_down: bfloat16 [4304, 1152], P('enc'), may hold values from -0.09375 to 0.09375
- cnx_in: bfloat16 [12288, 1536], P('dp'), may hold values from -6 to 6
- cnx_gain: float32 [1536], replicated, may hold values from 0.1 to 1.9
- cnx_up: bfloat16 [1536, 3072], P(None, 'enc'), may hold values from -0.15625 to 0.15625
- cnx_down: bfloat16 [3072, 1536], P('enc'), may hold values from -0.109375 to 0.109375
- pix_in: bfloat16 [12288, 1536], P('dp'), may hold values from -6 to 6
- pix_gain: float32 [1536], replicated, may hold values from 0.1 to 1.9
- pix_up: bfloat16 [1536, 3968], P(None, 'enc'), may hold values from -0.15625 to 0.15625
- pix_down: bfloat16 [3968, 1536], P('enc'), may hold values from -0.09375 to 0.09375
- proj_weight: bfloat16 [4224, 2048], P(None, 'enc'), may hold values from -0.09375 to 0.09375
- owners: int32 [3072, 1], P('dp'), may hold values from 0 to 31; in each aligned block of 96 rows (0 to 95, 96 to 191, ...) at most 6 rows name the same one
- cotangent: bfloat16 [32, 192, 2048], P('dp', None, 'enc'), may hold values from -0.59765625 to 0.59765625
Outputs:
- projected: bfloat16 [32, 192, 2048], P('dp', None, 'enc')
- grad_sig_up: float32 [1152, 4304], P('dp', 'enc')
- grad_sig_down: float32 [4304, 1152], P('enc', 'dp')
- grad_cnx_up: float32 [1536, 3072], P('dp', 'enc')
- grad_cnx_down: float32 [3072, 1536], P('enc', 'dp')
- grad_pix_up: float32 [1536, 3968], P('dp', 'enc')
- grad_pix_down: float32 [3968, 1536], P('enc', 'dp')
- grad_proj: float32 [4224, 2048], P('dp', 'enc')
The draws below stay inside these ranges and needn't reach their ends.
Inputs may be any that keep to these rules, and one draw needn't show every extreme that they name: `owners`: in each aligned block of 96 rows no owner is named by more than 6 rows, a bound that some block reaches.
All inputs are finite; a program needn't handle non-finite values.
Results may differ from the reference program's by a relative error of at most 0.0065.
Values may be sent and summed in bfloat16 or wider, within the bound.
A program may use at most 192 MiB of HBM per device.

```python
import math
import jax
import jax.numpy as jnp
import numpy as np
from jax import lax

SIG_D = 1152
SIG_H = 4304
CNX_D = 1536
CNX_H = 3072
PIX_D = 1536
PIX_H = 3968
LLM_W = 2048
GRID = 64
ROWS = 12288
POOL_DEV = 96
TOTAL_POOLED = 3072
CAT_D = 4224
CAP = 6
N_DP = 32


def with_spikes(array, stream_key, source, target, blocks, factor):
    owner, partner = [(jnp.arange(array.shape[axis_at]) // (array.shape[axis_at] // blocks)).reshape([-1 if axis == axis_at else 1 for axis in range(array.ndim)]) for axis_at in (source, target)]
    chosen = jax.random.permutation(stream_key, blocks)[partner]
    strong = (owner == chosen) | (owner == (partner + blocks // 2) % blocks)
    return jnp.where(strong, factor * array, array)


def levels(stream_key, extent, pieces, smallest, largest):
    def one(position, parts):
        draws = jax.random.uniform(jax.random.fold_in(jax.random.fold_in(stream_key, 6), position), (parts,), jnp.float32, smallest / len(pieces), largest / len(pieces))
        return jnp.repeat(jnp.exp(draws), extent[position] // parts).reshape((-1,) + (1,) * (len(extent) - position - 1))

    loudness = one(*pieces[0])
    for cut in pieces[1:]:
        loudness = loudness * one(*cut)
    return loudness


def deal_out(stream_key, own, number, rows, number_of, top, bound, skew):
    order = jax.random.permutation(stream_key, number_of)
    crowded, ordinary = shares(number_of, rows * top, bound, skew, True), shares(number_of, rows * top, bound, skew, False)
    places = jnp.arange(number_of)

    def named(sizes, rotation):
        used = int((sizes > 0).sum())
        fixed = max(1, used // 4)
        shifted = fixed + (places - fixed + rotation * (used - fixed)) % max(1, number_of - fixed)
        return jnp.zeros((number_of,), jnp.int32).at[order[jnp.where(places < fixed, places, shifted)]].set(jnp.asarray(sizes, jnp.int32))

    sizes = jnp.where(number % 4 == 0, named(crowded, number // 4), named(ordinary, number - number // 4 - 1))
    mixed = jax.random.permutation(jax.random.fold_in(own, 3), number_of)
    source_of, taker = mixed[0:number_of // 2 * 2:2], mixed[1:number_of // 2 * 2:2]
    margin = jnp.minimum(sizes[source_of] - 1, bound - sizes[taker]) // 2
    margin = jnp.where((source_of == order[0]) | (taker == order[0]) | (sizes[taker] == 0), 0, jnp.maximum(margin, 0))
    shifted = jax.random.randint(jax.random.fold_in(own, 4), (number_of // 2,), 0, 1 << 20) % (margin + 1)
    sizes = sizes.at[source_of].add(-shifted).at[taker].add(shifted)
    labels = jnp.searchsorted(jnp.cumsum(sizes), jnp.arange(rows * top), side="right").astype(jnp.int32)
    grid = labels.reshape(top, rows).T
    grid = grid[jax.random.permutation(jax.random.fold_in(own, 1), rows)]
    rotation = jax.random.randint(jax.random.fold_in(own, 2), (rows, 1), 0, top)
    return jnp.take_along_axis(grid, (jnp.arange(top)[None, :] + rotation) % top, axis=1)


def shares(amount, total, limit, skew, full):
    weights = [(1 << 20) // math.isqrt(standing ** skew) + 1 for standing in range(1, amount + 1)]
    largest = limit if full else min(limit, max(-(-total // amount), total * weights[0] // sum(weights)))
    least = 1 if total - largest >= amount - 1 else 0
    given, spare = [largest] + [least] * (amount - 1), total - largest - least * (amount - 1)
    while spare > 0:
        movable = [i for i in range(1, amount) if given[i] < largest] or [i for i in range(1, amount) if given[i] < limit]
        whole, remaining = sum([weights[i] for i in movable]), spare
        for i in movable:
            more = min(limit - given[i], max(1, remaining * weights[i] // whole), spare)
            given[i] = given[i] + more
            spare = spare - more
    return np.array(given)


def bell_draw(own_key, shape, width, limit, cuts=(), held_as=jnp.bfloat16):
    array = width * jax.random.normal(own_key, shape, jnp.float32)
    if cuts:
        array = array * levels(own_key, shape, cuts, -0.22, 0.18)
    return jnp.clip(array, -limit, limit).astype(held_as)


def noise_with(key, dims, scale, reach, cuts, heavy, kind=jnp.bfloat16):
    values = scale * jax.random.normal(key, dims, jnp.float32)
    if cuts:
        values = values * levels(key, dims, cuts, -0.22, 0.18)
    return jnp.clip(with_spikes(values, jax.random.fold_in(key, 3), *heavy), -reach, reach).astype(kind)


def setup_inputs(seed: int = 0) -> dict:
    keys = jax.random.split(jax.random.key(seed), 16)
    sig_in = noise_with(keys[0], (ROWS, SIG_D), 1.0, 6.0, ((0, 32),), (0, 1, 32, 2.75))
    sig_gain = jnp.clip(1.0 + 0.18 * jax.random.normal(keys[1], (SIG_D,), jnp.float32), 0.1, 1.9)
    sig_up = bell_draw(keys[2], (SIG_D, SIG_H), SIG_D ** -0.5, 0.1875, ((1, 4),))
    sig_down = bell_draw(keys[3], (SIG_H, SIG_D), SIG_H ** -0.5, 0.09375, ((0, 4),))
    cnx_in = noise_with(keys[4], (ROWS, CNX_D), 1.0, 6.0, ((0, 32),), (0, 1, 32, 2.75))
    cnx_gain = jnp.clip(1.0 + 0.18 * jax.random.normal(keys[5], (CNX_D,), jnp.float32), 0.1, 1.9)
    cnx_up = bell_draw(keys[6], (CNX_D, CNX_H), CNX_D ** -0.5, 0.15625, ((1, 4),))
    cnx_down = bell_draw(keys[7], (CNX_H, CNX_D), CNX_H ** -0.5, 0.109375, ((0, 4),))
    pix_in = noise_with(keys[8], (ROWS, PIX_D), 1.0, 6.0, ((0, 32),), (0, 1, 32, 2.75))
    pix_gain = jnp.clip(1.0 + 0.18 * jax.random.normal(keys[9], (PIX_D,), jnp.float32), 0.1, 1.9)
    pix_up = bell_draw(keys[10], (PIX_D, PIX_H), PIX_D ** -0.5, 0.15625, ((1, 4),))
    pix_down = bell_draw(keys[11], (PIX_H, PIX_D), PIX_H ** -0.5, 0.09375, ((0, 4),))
    proj_weight = bell_draw(keys[12], (CAT_D, LLM_W), CAT_D ** -0.5, 0.09375, ((1, 4),))
    owners_keys = jax.random.split(jax.random.fold_in(keys[13], 1), TOTAL_POOLED // POOL_DEV)
    owners_turns = jax.random.permutation(jax.random.fold_in(keys[13], 3), TOTAL_POOLED // POOL_DEV)
    owners = jax.vmap(lambda own, number: deal_out(jax.random.fold_in(keys[13], 2), own, number, POOL_DEV, N_DP, 1, CAP, 2))(owners_keys, owners_turns).reshape((TOTAL_POOLED, 1))
    cotangent = bell_draw(keys[14], (N_DP, N_DP * CAP, LLM_W), 0.1, 0.59765625, ((0, 32), (2, 4)))
    return {"sig_in": sig_in, "sig_gain": sig_gain, "sig_up": sig_up, "sig_down": sig_down, "cnx_in": cnx_in, "cnx_gain": cnx_gain, "cnx_up": cnx_up, "cnx_down": cnx_down, "pix_in": pix_in, "pix_gain": pix_gain, "pix_up": pix_up, "pix_down": pix_down, "proj_weight": proj_weight, "owners": owners, "cotangent": cotangent}


EPSILON = 1e-06

def normalize(inputs, norm_gain):
    widened = inputs.astype(jnp.float32)
    row_mean = lax.optimization_barrier(jnp.mean(widened, axis=1, keepdims=True))
    centered = widened - row_mean
    row_var = lax.optimization_barrier(jnp.mean(centered * centered, axis=1, keepdims=True))
    return (centered * lax.rsqrt(row_var + EPSILON) * norm_gain).astype(jnp.bfloat16)

def activate(values):
    return jax.nn.gelu(values, approximate=True)

def pool_grid(values):
    row_total, feat_width = values.shape
    blocks = values.reshape(row_total // (2 * GRID), 2, GRID // 2, 2, feat_width)
    return lax.optimization_barrier(jnp.mean(blocks, axis=(1, 3))).reshape(row_total // 4, feat_width)

def spread_grid(grads):
    pooled, feat_width = grads.shape
    blocks = grads.reshape(pooled // (GRID // 2), 1, GRID // 2, 1, feat_width)
    blocks = jnp.broadcast_to(blocks, (pooled // (GRID // 2), 2, GRID // 2, 2, feat_width))
    return blocks.reshape(pooled * 4, feat_width)

def full_product(left_side, right_side):
    return lax.dot_general(left_side, right_side, (((0,), (0,)), ((), ())), preferred_element_type=jnp.float32)

def reference(sig_in, sig_gain, sig_up, sig_down, cnx_in, cnx_gain, cnx_up, cnx_down, pix_in, pix_gain, pix_up, pix_down, proj_weight, owners, cotangent):
    encoders = ((sig_in, sig_gain, sig_up, sig_down), (cnx_in, cnx_gain, cnx_up, cnx_down), (pix_in, pix_gain, pix_up, pix_down))
    saved = []
    features = []
    for inputs, norm_gain, up_weight, down_weight in encoders:
        normed = normalize(inputs, norm_gain)
        hidden_pre = jnp.dot(normed, up_weight, preferred_element_type=jnp.float32)
        hidden_act = activate(hidden_pre).astype(jnp.bfloat16)
        branch = jnp.dot(hidden_act, down_weight, preferred_element_type=jnp.float32)
        features.append(pool_grid(inputs.astype(jnp.float32) + branch).astype(jnp.bfloat16))
        saved.append((normed, hidden_pre, hidden_act))
    concat = jnp.concatenate(features, axis=1)
    tokens = jnp.dot(concat, proj_weight, preferred_element_type=jnp.float32).astype(jnp.bfloat16)
    owner_ids = owners[:, 0].astype(jnp.int32)
    onehot = (owner_ids[:, None] == jnp.arange(N_DP, dtype=jnp.int32)[None, :]).astype(jnp.int32)
    blocks = onehot.reshape(N_DP, POOL_DEV, N_DP)
    before = (jnp.cumsum(blocks, axis=1).astype(jnp.int32) - blocks).astype(jnp.int32)
    slot_rank = lax.optimization_barrier(jnp.sum(blocks * before, axis=2)).reshape(-1).astype(jnp.int32)
    source = jnp.arange(TOTAL_POOLED, dtype=jnp.int32) // POOL_DEV
    flat_index = (owner_ids * (N_DP * CAP) + source * CAP + slot_rank).astype(jnp.int32)
    projected = jnp.zeros((N_DP * N_DP * CAP, LLM_W), jnp.bfloat16).at[flat_index].set(tokens)
    projected = projected.reshape(N_DP, N_DP * CAP, LLM_W)
    grad_tokens = cotangent.reshape(N_DP * N_DP * CAP, LLM_W)[flat_index]
    grad_proj = full_product(concat, grad_tokens)
    grad_concat = jnp.dot(grad_tokens, proj_weight.T, preferred_element_type=jnp.float32)
    offset = 0
    grads = []
    for encoder, stored in zip(encoders, saved):
        inputs, norm_gain, up_weight, down_weight = encoder
        normed, hidden_pre, hidden_act = stored
        feat_width = inputs.shape[1]
        grad_feat = grad_concat[:, offset:offset + feat_width]
        offset = offset + feat_width
        grad_branch = spread_grid(grad_feat * 0.25).astype(jnp.bfloat16)
        grad_act = jnp.dot(grad_branch, down_weight.T, preferred_element_type=jnp.float32)
        grad_pre = jax.vjp(activate, hidden_pre)[1](grad_act)[0].astype(jnp.bfloat16)
        grads.append(full_product(normed, grad_pre))
        grads.append(full_product(hidden_act, grad_branch))
    return (projected, grads[0], grads[1], grads[2], grads[3], grads[4], grads[5], grad_proj)
```

```python
import functools

import jax
import jax.numpy as jnp
from jax import lax
from jax.experimental import pallas as pl
from jax.experimental.pallas import tpu as pltpu
from jax.sharding import PartitionSpec as P

F32 = jnp.float32
BF16 = jnp.bfloat16
MESH = pl.DeviceIdType.MESH
EPSILON = 1e-06
GRID = 64
ROWS = 384
POOL = 96
CAT = 4224
LLM = 512
CAP = 6
PAD = 16
N_DP = 32
SLOTS = N_DP * PAD
PICK = 48
PROJ_CHUNK = 144
TILE = 256

ENCODERS = ((1152, 1076, 36, "z"), (1536, 768, 48, "y"), (1536, 992, 48, "z"))
OFFSETS = (0, 1152, 2688)
PARTS = (40, 48, 48)
CHUNKS = (80, 96, 96, PROJ_CHUNK)
LANES = (1152, 768, 1024, LLM)
FLIPPED = (True, False, True)
SIG, CNX, PIX = 0, 1, 2


def dot(left, right):
    return jnp.dot(left, right, preferred_element_type=F32)


def dot_nt(left, right):
    return lax.dot_general(left, right, (((1,), (1,)), ((), ())), preferred_element_type=F32)


def dot_tn(left, right):
    return lax.dot_general(left, right, (((0,), (0,)), ((), ())), preferred_element_type=F32)


def iota(shape, axis):
    return lax.broadcasted_iota(jnp.int32, shape, axis)


def tiles_of(extent, width):
    return [(start, min(width, extent - start)) for start in range(0, extent, width)]


def kernel(*refs):
    ins = refs[0:3]
    ups_hbm = refs[3:6]
    downs_hbm = refs[6:9]
    proj_hbm, cot_hbm, owners, *gains = refs[9:15]
    projected, *grads = refs[15:20]
    (
        normed_0, normed_1, normed_2, slope_0, slope_1, slope_2, pact_0, pact_1, pact_2,
        up_0, up_1, up_2, down_0, down_1, down_2, gfeat_0, gfeat_1, gfeat_2,
        land_0, land_1, land_2, land_3, cross_0, cross_1, cross_2, cross_3,
        proj, cot, spread, perm, place, out_buf, cot_in, tok_in, tok_grads,
        gpart, gpart_sib, gpart_far, bpart, bpart_sib, bpart_far, concat,
        cols_out, cols_in, choose,
        load_sem, a2a_send, a2a_recv, a2b_send, a2b_recv, gt_send, gt_recv, cols_send, cols_recv,
        colf_send, colf_recv, rows_send, rows_recv, sibs_send, sibs_recv, sum_send, sum_recv,
        gf_send, gf_recv, gfs_send, gfs_recv, rs_send, rs_recv, x_send, x_recv,
    ) = refs[20:]
    normed = (normed_0, normed_1, normed_2)
    slope = (slope_0, slope_1, slope_2)
    pact = (pact_0, pact_1, pact_2)
    up = (up_0, up_1, up_2)
    down = (down_0, down_1, down_2)
    gfeat = (gfeat_0, gfeat_1, gfeat_2)
    land = (land_0, land_1, land_2, land_3)
    cross = (cross_0, cross_1, cross_2, cross_3)

    enc = lax.axis_index("enc")
    dp = lax.axis_index("dp")
    core = lax.rem(enc, 2)
    x = lax.div(dp, 16)
    z = lax.rem(lax.div(dp, 4), 4)
    y = lax.rem(dp, 4)
    sibling = {"enc": enc + 1 - 2 * core, "dp": dp}
    far = {"enc": lax.rem(enc + 2, 4), "dp": dp}
    mirror = {"enc": enc, "dp": (1 - x) * 16 + z * 4 + y}
    position = {"z": z, "y": y}

    def step_to(axis, k):
        if axis == "z":
            return {"enc": enc, "dp": x * 16 + lax.rem(z + k, 4) * 4 + y}
        return {"enc": enc, "dp": x * 16 + z * 4 + lax.rem(y + k, 4)}

    sends = []
    row_sends = {}

    def remote(src, dst, send, recv, device):
        return pltpu.make_async_remote_copy(
            src_ref=src, dst_ref=dst, send_sem=send, recv_sem=recv, device_id=device,
            device_id_type=MESH,
        )

    def send(src, dst, send_sem, recv_sem, device):
        copy = remote(src, dst, send_sem, recv_sem, device)
        copy.start()
        sends.append(copy)
        return copy

    barrier = pltpu.get_barrier_semaphore()

    def greet(k, carry):
        other = {"enc": enc, "dp": lax.rem(dp + k, N_DP)}
        pl.semaphore_signal(barrier, inc=1, device_id=other, device_id_type=MESH)
        return carry

    lax.fori_loop(1, N_DP, greet, 0)
    for other in (sibling, far):
        pl.semaphore_signal(barrier, inc=1, device_id=other, device_id_type=MESH)

    loads = {}

    def load(name, src, dst):
        copy = pltpu.make_async_copy(src, dst, load_sem.at[len(loads)])
        copy.start()
        loads[name] = copy

    load("cot", cot_hbm.at[0], cot)
    for i in (CNX, PIX, SIG):
        load(f"in{i}", ins[i], normed[i].at[position[ENCODERS[i][3]]])
    load("proj", proj_hbm, proj)
    for i in (CNX, PIX, SIG):
        load(f"up{i}", ups_hbm[i], up[i])
    for i in (CNX, PIX, SIG):
        load(f"down{i}", downs_hbm[i], down[i])

    row = iota((ROWS, ROWS), 0)
    col = iota((ROWS, ROWS), 1)
    for q in range(4):
        pooled = iota((POOL, ROWS), 0)
        origin = lax.shift_right_logical(pooled, 5) * 128 + (q // 2) * 64
        origin = origin + lax.bitwise_and(pooled, 31) * 2 + q % 2
        perm[q * POOL:(q + 1) * POOL, :] = (iota((POOL, ROWS), 1) == origin).astype(BF16)
    del row, col

    wide = iota((N_DP * CAP, SLOTS), 1)
    rank = lax.bitwise_and(wide, PAD - 1)
    target = lax.shift_right_logical(wide, 4) * CAP + rank
    spread[...] = ((iota((N_DP * CAP, SLOTS), 0) == target) & (rank < CAP)).astype(BF16)

    owner_ids = owners[...]
    onehot = (owner_ids == iota((POOL, 128), 1)).astype(F32)
    earlier = (iota((POOL, POOL), 1) < iota((POOL, POOL), 0)).astype(BF16)
    before = dot(earlier, onehot.astype(BF16))
    slot_rank = jnp.sum(onehot * before, axis=1, keepdims=True)
    slot = owner_ids.astype(F32) * float(PAD) + slot_rank
    place[...] = (iota((POOL, SLOTS), 1).astype(F32) == slot).astype(BF16)

    loads["cot"].wait()
    out_buf[...] = dot_tn(spread[...], cot[...]).astype(BF16)

    def normalize(i):
        width, _, _, axis = ENCODERS[i]
        own = normed[i].at[position[axis]]
        loads[f"in{i}"].wait()
        for start, size in tiles_of(width, 384):
            block = own[:, start:start + size]
            own[:, start:start + size] = dot(perm[...], block).astype(BF16)
        gain = gains[i][...]

        def part(k, carry):
            rows = pl.ds(pl.multiple_of(k * 32, 32), 32)
            total = jnp.zeros((32, width), F32)
            for q in range(4):
                cells = pl.ds(pl.multiple_of(q * POOL + k * 32, 32), 32)
                values = own[cells, :].astype(F32)
                total = total + values
                mean = jnp.mean(values, axis=1, keepdims=True)
                centered = values - mean
                var = jnp.mean(centered * centered, axis=1, keepdims=True)
                own[cells, :] = (centered * lax.rsqrt(var + EPSILON) * gain).astype(BF16)
            bpart[rows, OFFSETS[i]:OFFSETS[i] + width] = (total * 0.0625).astype(BF16)
            return carry

        lax.fori_loop(0, POOL // 32, part, 0)

    half = pl.ds(pl.multiple_of(core * 192, 192), 192)
    plane_a = pl.ds(pl.multiple_of(core * 192, 96), POOL)
    plane_b = pl.ds(pl.multiple_of(core * 192 + POOL, 96), POOL)

    def rows_start(i):
        axis = ENCODERS[i][3]
        p = position[axis]
        block = normed[i].at[p, half]
        row_sends[i] = [
            remote(block, block, rows_send.at[i, 0], rows_recv.at[i, 0], step_to(axis, 1)),
            remote(block, block, rows_send.at[i, 1], rows_recv.at[i, 1], step_to(axis, 3)),
        ]
        for copy in row_sends[i]:
            copy.start()

    def rows_relay(i):
        axis = ENCODERS[i][3]
        p = position[axis]
        before_me = normed[i].at[lax.rem(p + 3, 4)]
        after_me = normed[i].at[lax.rem(p + 1, 4)]
        block = before_me.at[half]
        remote(block, block, rows_send.at[i, 0], rows_recv.at[i, 0], step_to(axis, 1)).wait_recv()
        part = before_me.at[plane_a]
        send(part, part, rows_send.at[i, 2], rows_recv.at[i, 2], step_to(axis, 1))
        send(block, block, sibs_send.at[i, 0], sibs_recv.at[i, 0], sibling)
        block = after_me.at[half]
        remote(block, block, rows_send.at[i, 1], rows_recv.at[i, 1], step_to(axis, 3)).wait_recv()
        part = after_me.at[plane_b]
        send(part, part, rows_send.at[i, 3], rows_recv.at[i, 3], step_to(axis, 3))
        send(block, block, sibs_send.at[i, 1], sibs_recv.at[i, 1], sibling)

    def rows_last(i):
        axis = ENCODERS[i][3]
        p = position[axis]
        opposite = normed[i].at[lax.rem(p + 2, 4)]
        part = opposite.at[plane_a]
        remote(part, part, rows_send.at[i, 2], rows_recv.at[i, 2], step_to(axis, 1)).wait_recv()
        part = opposite.at[plane_b]
        remote(part, part, rows_send.at[i, 3], rows_recv.at[i, 3], step_to(axis, 3)).wait_recv()
        block = opposite.at[half]
        send(block, block, sibs_send.at[i, 2], sibs_recv.at[i, 2], sibling)

    other_half = pl.ds(pl.multiple_of((1 - core) * 192, 192), 192)

    def rows_wait(i, k):
        p = position[ENCODERS[i][3]]
        block = normed[i].at[lax.rem(p + (3, 1, 2)[k], 4), other_half]
        remote(block, block, sibs_send.at[i, k], sibs_recv.at[i, k], sibling).wait_recv()

    def forward(i, source):
        _, hidden, _, _ = ENCODERS[i]
        pooled_rows = pl.ds(pl.multiple_of(source * POOL, POOL), POOL)
        for start, size in tiles_of(hidden, TILE):
            cols = slice(start, start + size)
            if FLIPPED[i]:
                pre = dot_nt(normed[i][source], up[i][cols, :])
            else:
                pre = dot(normed[i][source], up[i][:, cols])
            square = pre * pre
            inner = pre * (0.7978845608028654 + 0.035677408136300125 * square)
            tanh = jnp.tanh(inner)
            upper = 0.5 + 0.5 * tanh
            act = pre * upper
            act_16 = act.astype(BF16)
            grow = 0.7978845608028654 + 0.10703222440890037 * square
            slope[i][source, :, cols] = (upper + act * (1.0 - tanh) * grow).astype(BF16)
            wide_act = act_16.astype(F32)
            total = (wide_act[0:96] + wide_act[96:192]) + (wide_act[192:288] + wide_act[288:384])
            pact[i][pooled_rows, cols] = total.astype(BF16)

    def branch(i):
        width, _, _, axis = ENCODERS[i]
        rows = pl.ds(pl.multiple_of(position[axis] * POOL, POOL), POOL)
        for start, size in tiles_of(width, 384):
            cols = slice(OFFSETS[i] + start, OFFSETS[i] + start + size)
            value = dot(pact[i][rows, :], down[i][:, start:start + size]) * 0.25
            bpart[:, cols] = (bpart[:, cols].astype(F32) + value).astype(BF16)

    mine = pl.ds(pl.multiple_of(core * 48, 48), 48)
    theirs = pl.ds(pl.multiple_of(48 - core * 48, 48), 48)

    def sum_start(n, part, near):
        send(part.at[theirs], near, sum_send.at[n, 0], sum_recv.at[n, 0], sibling)

    def sum_cross(n, part, near, distant):
        remote(part.at[theirs], near, sum_send.at[n, 0], sum_recv.at[n, 0], sibling).wait_recv()
        part[mine, :] = (part[mine, :].astype(F32) + near[...].astype(F32)).astype(BF16)
        send(part.at[mine], distant, sum_send.at[n, 1], sum_recv.at[n, 1], far)

    def sum_wait(n, part, distant):
        remote(part.at[mine], distant, sum_send.at[n, 1], sum_recv.at[n, 1], far).wait_recv()

    def gfeat_finish():
        sum_wait(0, gpart, gpart_far)
        for i in (CNX, PIX, SIG):
            width, _, _, axis = ENCODERS[i]
            p = position[axis]
            cols = slice(OFFSETS[i], OFFSETS[i] + width)
            total = gpart[mine, cols].astype(F32) + gpart_far[:, cols].astype(F32)
            rows = pl.ds(pl.multiple_of(p * POOL + core * 48, 48), 48)
            gfeat[i][rows, :] = total.astype(BF16)
            block = gfeat[i].at[rows]
            for k in (1, 3, 2):
                send(block, block, gf_send.at[i, k], gf_recv.at[i, k], step_to(axis, k))
            send(block, block, gfs_send.at[i, 0], gfs_recv.at[i, 0], sibling)

    def gfeat_relay(i):
        axis = ENCODERS[i][3]
        p = position[axis]
        for k in (1, 3, 2):
            rows = pl.ds(pl.multiple_of(lax.rem(p + 4 - k, 4) * POOL + core * 48, 48), 48)
            block = gfeat[i].at[rows]
            remote(block, block, gf_send.at[i, k], gf_recv.at[i, k], step_to(axis, k)).wait_recv()
            send(block, block, gfs_send.at[i, k], gfs_recv.at[i, k], sibling)

    def gfeat_wait(i):
        p = position[ENCODERS[i][3]]
        for k in range(4):
            rows = pl.ds(pl.multiple_of(lax.rem(p + 4 - k, 4) * POOL + 48 - core * 48, 48), 48)
            block = gfeat[i].at[rows]
            remote(block, block, gfs_send.at[i, k], gfs_recv.at[i, k], sibling).wait_recv()

    def concat_finish():
        sum_wait(1, bpart, bpart_far)
        total = bpart[mine, :].astype(F32) + bpart_far[...].astype(F32)
        concat[mine, :] = total.astype(BF16)
        block = concat.at[mine]
        send(block, block, sum_send.at[1, 2], sum_recv.at[1, 2], sibling)

    def concat_wait():
        block = concat.at[theirs]
        remote(block, block, sum_send.at[1, 2], sum_recv.at[1, 2], sibling).wait_recv()

    def exchange(dst, send_sem, recv_sem):
        def one(k, carry):
            other = lax.rem(dp + k, N_DP)
            src = out_buf.at[pl.ds(pl.multiple_of(other * PAD, PAD), PAD)]
            to = dst.at[pl.ds(pl.multiple_of(dp * PAD, PAD), PAD)]
            device = {"enc": enc, "dp": other}
            remote(src, to, send_sem.at[k], recv_sem.at[k], device).start()
            return carry

        lax.fori_loop(1, N_DP, one, 0)
        here = pl.ds(pl.multiple_of(dp * PAD, PAD), PAD)
        dst[here, :] = out_buf[here, :]

    def exchange_wait(dst, send_sem, recv_sem, arrived):
        def one(k, carry):
            other = lax.rem(dp + k, N_DP) if not arrived else lax.rem(dp + N_DP - k, N_DP)
            src = out_buf.at[pl.ds(pl.multiple_of(other * PAD, PAD), PAD)]
            to = dst.at[pl.ds(pl.multiple_of(other * PAD, PAD), PAD)]
            device = {"enc": enc, "dp": other}
            copy = remote(src, to, send_sem.at[k], recv_sem.at[k], device)
            if arrived:
                copy.wait_recv()
            else:
                copy.wait_send()
            return carry

        lax.fori_loop(1, N_DP, one, 0)

    hold = up + (proj,)
    lanes = tuple(slice(0, w) for w in LANES)

    def backward(i):
        width, hidden, rows_out, axis = ENCODERS[i]
        p = position[axis]
        for k in range(8):
            b, xx = k // 2, k % 2
            index = xx * 16 + (b * 4 + p if axis == "y" else p * 4 + b)
            r = iota((PICK, width), 0)
            hit = (iota((PICK, width), 1) == r + index * rows_out) & (r < rows_out)
            choose[k * PICK:(k + 1) * PICK, 0:width] = hit.astype(BF16)
        chosen = choose[:, 0:width]
        order = [lax.rem(p + s, 4) for s in range(4)]
        stage = CNX if i == SIG else i
        if i != SIG:
            for copy in row_sends[i]:
                copy.wait_send()
        picked = normed[stage].at[position[ENCODERS[stage][3]]]
        for s in range(4):
            block = dot_nt(chosen, normed[i][order[s]]).astype(BF16)
            picked[:, s * ROWS:(s + 1) * ROWS] = block
        gpicked = perm
        gpicked[...] = dot_nt(chosen, gfeat[i][...]).astype(BF16)
        for start, size in tiles_of(hidden, TILE):
            cols = slice(start, start + size)
            grad_act = dot_nt(gfeat[i][...], down[i][cols, :])
            for s in range(4):
                grad = grad_act[s * POOL:(s + 1) * POOL]
                for q in range(4):
                    cells = slice(q * POOL, (q + 1) * POOL)
                    value = slope[i][s, cells, cols].astype(F32) * grad
                    slope[i][s, cells, cols] = value.astype(BF16)
            upper = dot(picked[:, 0:ROWS], slope[i][order[0], :, cols])
            for s in range(1, 4):
                upper = upper + dot(picked[:, s * ROWS:(s + 1) * ROWS], slope[i][order[s], :, cols])
            lower = dot(gpicked[...], pact[i][:, cols])
            part = PARTS[i]
            for k in range(8):
                rows = slice(k * PICK, k * PICK + part)
                both = jnp.concatenate([upper[rows], lower[rows]], axis=0).astype(BF16)
                hold[i][2 * k * part:2 * (k + 1) * part, cols] = both

    ring = ("y", "z", "y", "z")

    def chunk(n, b, xx):
        size = CHUNKS[n]
        return pl.ds(pl.multiple_of((b * 2 + xx) * size, size), size)

    def ring_copy(n, k):
        axis = ring[n]
        p = position[axis]
        nxt, opp, prv = lax.rem(p + 1, 4), lax.rem(p + 2, 4), lax.rem(p + 3, 4)
        where = ((opp, 0), (opp, 1), (nxt, 1), (prv, 0), (nxt, 0), (prv, 1))[k]
        device = step_to(axis, 1 if k in (0, 2, 4) else 3)
        src = hold[n].at[chunk(n, *where), lanes[n]]
        return remote(src, land[n].at[k], rs_send.at[n, k], rs_recv.at[n, k], device)

    def reduce_start(n):
        for k in range(4):
            copy = ring_copy(n, k)
            copy.start()
            sends.append(copy)

    def reduce_mid(n):
        p = position[ring[n]]
        for k, b, xx in ((0, lax.rem(p + 1, 4), 0), (1, lax.rem(p + 3, 4), 1)):
            ring_copy(n, k).wait_recv()
            rows = chunk(n, b, xx)
            total = hold[n][rows, lanes[n]].astype(F32) + land[n][k].astype(F32)
            hold[n][rows, lanes[n]] = total.astype(BF16)
            copy = ring_copy(n, 4 + k)
            copy.start()
            sends.append(copy)

    def cross_copy(n):
        p = position[ring[n]]
        src = hold[n].at[chunk(n, p, 1 - x), lanes[n]]
        return remote(src, cross[n], x_send.at[n], x_recv.at[n], mirror)

    def reduce_cross(n):
        p = position[ring[n]]
        for k in range(2, 6):
            ring_copy(n, k).wait_recv()

        def total(xx):
            value = hold[n][chunk(n, p, xx), lanes[n]].astype(F32) + land[n][3 - xx].astype(F32)
            return value + land[n][4 + xx].astype(F32)

        hold[n][chunk(n, p, 1 - x), lanes[n]] = total(1 - x).astype(BF16)
        copy = cross_copy(n)
        copy.start()
        sends.append(copy)
        grads[n][...] = total(x)

    def reduce_end(n):
        cross_copy(n).wait_recv()
        grads[n][...] = grads[n][...] + cross[n][...].astype(F32)

    def columns(a):
        def one(j, out):
            k = core * 4 + j
            index = lax.rem(k, 2) * 16 + lax.div(k, 2) * 4 + a
            r = iota((PROJ_CHUNK, 256), 0)
            hit = (iota((PROJ_CHUNK, 256), 1) == r + index * 4) & (r < 132)
            window = concat[:, pl.ds(pl.multiple_of(index * 128, 128), 256)]
            return dot_nt(hit.astype(BF16), window).astype(BF16)

        return one

    col_half = pl.ds(pl.multiple_of(core * 576, 576), 576)
    col_other = pl.ds(pl.multiple_of(576 - core * 576, 576), 576)

    def lane(pos):
        return pl.ds(pl.multiple_of(pos * 128, 128), 128)

    def columns_start():
        for k in range(1, 4):
            one = columns(lax.rem(y + k, 4))

            def fill(j, carry, k=k, one=one):
                rows = pl.ds(pl.multiple_of(j * PROJ_CHUNK, PROJ_CHUNK), PROJ_CHUNK)
                cols_out[k - 1, rows, :] = one(j, None)
                return carry

            lax.fori_loop(0, 4, fill, 0)
            send(cols_out.at[k - 1], cols_in.at[col_half, lane(y)], cols_send.at[k],
                 cols_recv.at[k], step_to("y", k))
        one = columns(y)

        def fill_own(j, carry):
            rows = pl.ds(pl.multiple_of((core * 4 + j) * PROJ_CHUNK, PROJ_CHUNK), PROJ_CHUNK)
            cols_in[rows, lane(y)] = one(j, None)
            return carry

        lax.fori_loop(0, 4, fill_own, 0)
        block = cols_in.at[col_half, lane(y)]
        send(block, block, colf_send.at[0], colf_recv.at[0], sibling)

    def columns_relay():
        for k in range(1, 4):
            block = cols_in.at[col_half, lane(lax.rem(y + 4 - k, 4))]
            remote(cols_out.at[k - 1], block, cols_send.at[k], cols_recv.at[k],
                   step_to("y", k)).wait_recv()
            send(block, block, colf_send.at[k], colf_recv.at[k], sibling)

    def columns_wait():
        for k in range(4):
            block = cols_in.at[col_other, lane(lax.rem(y + 4 - k, 4))]
            remote(block, block, colf_send.at[k], colf_recv.at[k], sibling).wait_recv()

    def token_rows(pos):
        return tok_grads.at[pl.ds(pl.multiple_of(pos * 128, 128), 128)]

    normalize(CNX)
    pl.semaphore_wait(barrier, N_DP + 1)
    exchange(cot_in, a2a_send, a2a_recv)
    rows_start(CNX)
    normalize(PIX)
    rows_start(PIX)
    normalize(SIG)
    rows_start(SIG)

    loads["proj"].wait()
    exchange_wait(cot_in, a2a_send, a2a_recv, True)
    own_grads = dot(place[...], cot_in[...]).astype(BF16)
    tok_grads[pl.ds(pl.multiple_of(y * 128, 128), 128), :] = jnp.concatenate(
        [own_grads, jnp.zeros((32, LLM), BF16)], axis=0
    )
    for k in range(1, 4):
        send(token_rows(y), token_rows(y), gt_send.at[k], gt_recv.at[k], step_to("y", k))
    for start, size in tiles_of(CAT, 384):
        rows = tok_grads[pl.ds(pl.multiple_of(y * 128, 32), POOL), :]
        gpart[:, start:start + size] = (dot_nt(rows, proj[start:start + size, :]) * 0.25).astype(BF16)
    sum_start(0, gpart, gpart_sib)

    loads[f"up{CNX}"].wait()
    forward(CNX, y)
    sum_cross(0, gpart, gpart_sib, gpart_far)
    loads[f"up{PIX}"].wait()
    forward(PIX, z)
    loads[f"up{SIG}"].wait()
    forward(SIG, z)
    for i in (CNX, PIX, SIG):
        loads[f"down{i}"].wait()
        branch(i)
    sum_start(1, bpart, bpart_sib)
    sum_cross(1, bpart, bpart_sib, bpart_far)

    for i in (CNX, PIX, SIG):
        rows_relay(i)
    gfeat_finish()
    concat[POOL:128, :] = jnp.zeros((32, CAT), BF16)

    def forward_rest(i, first, last):
        p = position[ENCODERS[i][3]]

        def one(k, carry):
            forward(i, lax.rem(p + k, 4))
            return carry

        lax.fori_loop(first, last, one, 0)

    for i in (CNX, PIX, SIG):
        rows_wait(i, 0)
        rows_wait(i, 1)
    for i in (CNX, PIX, SIG):
        p = position[ENCODERS[i][3]]

        def near(k, carry, i=i, p=p):
            forward(i, lax.rem(p + 1 + 2 * k, 4))
            return carry

        lax.fori_loop(0, 2, near, 0)
        rows_last(i)
    concat_finish()
    for i in (CNX, PIX, SIG):
        gfeat_relay(i)
    concat_wait()

    exchange_wait(cot_in, a2a_send, a2a_recv, False)
    tokens = jnp.zeros((POOL, LLM), F32)
    for start, size in tiles_of(CAT, 384):
        tokens = tokens + dot(concat[0:POOL, start:start + size], proj[start:start + size, :])
    out_buf[...] = dot_tn(place[...], tokens.astype(BF16)).astype(BF16)
    exchange(tok_in, a2b_send, a2b_recv)
    columns_start()

    for i in (CNX, PIX, SIG):
        rows_wait(i, 2)
        gfeat_wait(i)
        forward(i, lax.rem(position[ENCODERS[i][3]] + 2, 4))
        backward(i)
        reduce_start(i)
    columns_relay()
    reduce_mid(CNX)
    for k in range(1, 4):
        remote(token_rows(y), token_rows(lax.rem(y + 4 - k, 4)), gt_send.at[k], gt_recv.at[k],
               step_to("y", k)).wait_recv()
    columns_wait()
    for k in range(8):
        rows = slice(k * PROJ_CHUNK, (k + 1) * PROJ_CHUNK)
        proj[rows, :] = dot(cols_in[rows, :], tok_grads[...]).astype(BF16)
    reduce_start(3)
    reduce_mid(PIX)
    reduce_cross(CNX)
    reduce_mid(SIG)
    exchange_wait(tok_in, a2b_send, a2b_recv, True)
    projected[...] = dot(spread[...], tok_in[...]).astype(BF16)
    reduce_mid(3)
    reduce_cross(PIX)
    reduce_cross(SIG)
    reduce_cross(3)
    for n in (CNX, PIX, SIG, 3):
        reduce_end(n)

    exchange_wait(tok_in, a2b_send, a2b_recv, False)
    for copy in sends + row_sends[SIG]:
        copy.wait_send()


def local(
    sig_in, sig_gain, sig_up, sig_down, cnx_in, cnx_gain, cnx_up, cnx_down,
    pix_in, pix_gain, pix_up, pix_down, proj_weight, owners, cotangent,
):
    any_spec = pl.BlockSpec(memory_space=pl.ANY)
    vmem_spec = pl.BlockSpec(memory_space=pltpu.VMEM)
    vmem = pltpu.VMEM
    dma = pltpu.SemaphoreType.DMA
    widths = [e[0] for e in ENCODERS]
    hiddens = [e[1] for e in ENCODERS]
    scratch = (
        [vmem((4, ROWS, w), BF16) for w in widths]
        + [vmem((4, ROWS, h), BF16) for h in hiddens]
        + [vmem((4 * POOL, h), BF16) for h in hiddens]
        + [vmem((h, w) if f else (w, h), BF16) for w, h, f in zip(widths, hiddens, FLIPPED)]
        + [vmem((h, w), BF16) for w, h in zip(widths, hiddens)]
        + [vmem((4 * POOL, w), BF16) for w in widths]
        + [vmem((6, c, w), BF16) for c, w in zip(CHUNKS, LANES)]
        + [vmem((c, w), BF16) for c, w in zip(CHUNKS, LANES)]
        + [
            vmem((CAT, LLM), BF16),
            vmem((N_DP * CAP, LLM), BF16),
            vmem((N_DP * CAP, SLOTS), BF16),
            vmem((ROWS, ROWS), BF16),
            vmem((POOL, SLOTS), BF16),
            vmem((SLOTS, LLM), BF16),
            vmem((SLOTS, LLM), BF16),
            vmem((SLOTS, LLM), BF16),
            vmem((SLOTS, LLM), BF16),
            vmem((POOL, CAT), BF16),
            vmem((POOL // 2, CAT), BF16),
            vmem((POOL // 2, CAT), BF16),
            vmem((POOL, CAT), BF16),
            vmem((POOL // 2, CAT), BF16),
            vmem((POOL // 2, CAT), BF16),
            vmem((128, CAT), BF16),
            vmem((3, 4 * PROJ_CHUNK, 128), BF16),
            vmem((8 * PROJ_CHUNK, LLM), BF16),
            vmem((8 * PICK, 1536), BF16),
        ]
        + [
            dma((11,)),
            dma((N_DP,)), dma((N_DP,)), dma((N_DP,)), dma((N_DP,)),
            dma((4,)), dma((4,)), dma((4,)), dma((4,)), dma((4,)), dma((4,)),
            dma((3, 4)), dma((3, 4)), dma((3, 3)), dma((3, 3)),
            dma((2, 3)), dma((2, 3)),
            dma((3, 4)), dma((3, 4)), dma((3, 4)), dma((3, 4)),
            dma((4, 6)), dma((4, 6)), dma((4,)), dma((4,)),
        ]
    )
    outs = pl.pallas_call(
        kernel,
        out_shape=[
            jax.ShapeDtypeStruct((N_DP * CAP, LLM), BF16),
            *[jax.ShapeDtypeStruct((c, w), F32) for c, w in zip(CHUNKS, LANES)],
        ],
        in_specs=[any_spec] * 11 + [vmem_spec] * 4,
        out_specs=[vmem_spec] * 5,
        scratch_shapes=scratch,
        compiler_params=pltpu.CompilerParams(
            collective_id=0, has_side_effects=True, vmem_limit_bytes=64 * 2**20
        ),
        cost_estimate=pl.CostEstimate(flops=2 * 10**10, bytes_accessed=3 * 10**7, transcendentals=0),
    )(
        sig_in, cnx_in, pix_in, sig_up.T, cnx_up, pix_up.T, sig_down, cnx_down, pix_down,
        proj_weight, cotangent, owners,
        sig_gain.reshape(1, -1), cnx_gain.reshape(1, -1), pix_gain.reshape(1, -1),
    )
    results = [outs[0][None]]
    for i in (SIG, CNX, PIX):
        rows_out = ENCODERS[i][2]
        results.append(outs[1 + i][0:rows_out, 0:hiddens[i]])
        results.append(outs[1 + i][PARTS[i]:PARTS[i] + rows_out, 0:hiddens[i]].T)
    results.append(outs[4][0:132])
    return tuple(results)


def solution(mesh):
    placed = (
        P("dp", None), P(), P(None, "enc"), P("enc", None),
        P("dp", None), P(), P(None, "enc"), P("enc", None),
        P("dp", None), P(), P(None, "enc"), P("enc", None),
        P(None, "enc"), P("dp", None), P("dp", None, "enc"),
    )
    return jax.shard_map(
        local,
        mesh=mesh,
        in_specs=placed,
        out_specs=(
            P("dp", None, "enc"), P("dp", "enc"), P("enc", "dp"), P("dp", "enc"),
            P("enc", "dp"), P("dp", "enc"), P("enc", "dp"), P("dp", "enc"),
        ),
        check_vma=False,
    )
```

```python
import functools

import jax
import jax.numpy as jnp
from jax import lax
from jax.experimental import pallas as pl
from jax.experimental.pallas import tpu as pltpu
from jax.sharding import PartitionSpec as P

F32 = jnp.float32
BF16 = jnp.bfloat16
MESH = pl.DeviceIdType.MESH
EPSILON = 1e-06
GRID = 64
ROWS = 384
POOL = 96
CAT = 4224
LLM = 512
CAP = 6
PAD = 16
N_DP = 32
SLOTS = N_DP * PAD
PICK = 48
PROJ_CHUNK = 144
TILE = 256

ENCODERS = ((1152, 1076, 36, "z"), (1536, 768, 48, "y"), (1536, 992, 48, "z"))
OFFSETS = (0, 1152, 2688)
PARTS = (40, 48, 48)
CHUNKS = (80, 96, 96, PROJ_CHUNK)
UNITS = ((0, 0, 512), (0, 512, 640), (1, 0, 768), (2, 0, 512), (2, 512, 512), (3, 0, LLM))
SIG_A, SIG_B, CNX_A, PIX_A, PIX_B, PROJ_A = range(6)
FROM = (0, 2, 3, 1)
FLIPPED = (True, False, True)
SIG, CNX, PIX = 0, 1, 2


def dot(left, right):
    return jnp.dot(left, right, preferred_element_type=F32)


def dot_nt(left, right):
    return lax.dot_general(left, right, (((1,), (1,)), ((), ())), preferred_element_type=F32)


def dot_tn(left, right):
    return lax.dot_general(left, right, (((0,), (0,)), ((), ())), preferred_element_type=F32)


def iota(shape, axis):
    return lax.broadcasted_iota(jnp.int32, shape, axis)


def tiles_of(extent, width):
    return [(start, min(width, extent - start)) for start in range(0, extent, width)]


def kernel(*refs):
    ins = refs[0:3]
    ups_hbm = refs[3:6]
    downs_hbm = refs[6:9]
    proj_hbm, cot_hbm, owners, *gains = refs[9:15]
    projected = refs[15]
    grads = ((refs[16], refs[17]), (refs[18], refs[19]), (refs[20], refs[21]), (refs[22],))
    (
        normed_0, normed_1, normed_2, slope_0, slope_1, slope_2, pact_0, pact_1, pact_2,
        up_0, up_1, up_2, down_0, down_1, down_2, gfeat_0, gfeat_1, gfeat_2,
        land_0, land_1, land_2, land_3, land_4, land_5,
        cross_0, cross_1, cross_2, cross_3, cross_4, cross_5,
        proj, cot, spread, perm, place, out_buf, cot_in, tok_in, tok_grads,
        gpart, gpart_sib, gpart_far, bpart, bpart_sib, bpart_far, concat,
        cols_out, cols_in, choose, picked,
        load_sem, a2a_send, a2a_recv, a2b_send, a2b_recv, gt_send, gt_recv, cols_send, cols_recv,
        colf_send, colf_recv, rows_send, rows_recv, sibs_send, sibs_recv, sum_send, sum_recv,
        gf_send, gf_recv, gfs_send, gfs_recv, rs_send, rs_recv, x_send, x_recv,
    ) = refs[23:]
    normed = (normed_0, normed_1, normed_2)
    slope = (slope_0, slope_1, slope_2)
    pact = (pact_0, pact_1, pact_2)
    up = (up_0, up_1, up_2)
    down = (down_0, down_1, down_2)
    gfeat = (gfeat_0, gfeat_1, gfeat_2)
    land = (land_0, land_1, land_2, land_3, land_4, land_5)
    cross = (cross_0, cross_1, cross_2, cross_3, cross_4, cross_5)

    enc = lax.axis_index("enc")
    dp = lax.axis_index("dp")
    core = lax.rem(enc, 2)
    x = lax.div(dp, 16)
    z = lax.rem(lax.div(dp, 4), 4)
    y = lax.rem(dp, 4)
    sibling = {"enc": enc + 1 - 2 * core, "dp": dp}
    far = {"enc": lax.rem(enc + 2, 4), "dp": dp}
    mirror = {"enc": enc, "dp": (1 - x) * 16 + z * 4 + y}
    position = {"z": z, "y": y}

    def step_to(axis, k):
        if axis == "z":
            return {"enc": enc, "dp": x * 16 + lax.rem(z + k, 4) * 4 + y}
        return {"enc": enc, "dp": x * 16 + z * 4 + lax.rem(y + k, 4)}

    sends = []

    def remote(src, dst, send, recv, device):
        return pltpu.make_async_remote_copy(
            src_ref=src, dst_ref=dst, send_sem=send, recv_sem=recv, device_id=device,
            device_id_type=MESH,
        )

    def send(src, dst, send_sem, recv_sem, device):
        copy = remote(src, dst, send_sem, recv_sem, device)
        copy.start()
        sends.append(copy)
        return copy

    barrier = pltpu.get_barrier_semaphore()

    def greet(k, carry):
        other = {"enc": enc, "dp": lax.rem(dp + k, N_DP)}
        pl.semaphore_signal(barrier, inc=1, device_id=other, device_id_type=MESH)
        return carry

    lax.fori_loop(1, N_DP, greet, 0)
    for other in (sibling, far):
        pl.semaphore_signal(barrier, inc=1, device_id=other, device_id_type=MESH)

    loads = {}

    def load(name, src, dst):
        copy = pltpu.make_async_copy(src, dst, load_sem.at[len(loads)])
        copy.start()
        loads[name] = copy

    load("cot", cot_hbm.at[0], cot)
    for i in (CNX, PIX, SIG):
        load(f"in{i}", ins[i], normed[i].at[0])
    load("proj", proj_hbm, proj)
    for i in (CNX, PIX, SIG):
        load(f"up{i}", ups_hbm[i], up[i])
    for i in (CNX, PIX, SIG):
        load(f"down{i}", downs_hbm[i], down[i])

    for q in range(4):
        pooled = iota((POOL, ROWS), 0)
        origin = lax.shift_right_logical(pooled, 5) * 128 + (q // 2) * 64
        origin = origin + lax.bitwise_and(pooled, 31) * 2 + q % 2
        perm[q * POOL:(q + 1) * POOL, :] = (iota((POOL, ROWS), 1) == origin).astype(BF16)

    wide = iota((N_DP * CAP, SLOTS), 1)
    for h in range(2):
        rank = lax.bitwise_and(wide, PAD - 1) - 8 * h
        target = lax.shift_right_logical(wide, 4) * CAP + rank
        hit = (iota((N_DP * CAP, SLOTS), 0) == target) & (rank >= 0) & (rank < CAP)
        spread[h] = hit.astype(BF16)

    diagonal = iota((POOL, POOL), 0) == iota((POOL, POOL), 1)
    owner_ids = jnp.sum(jnp.where(diagonal, owners[...], 0), axis=1, keepdims=True)
    onehot = (owner_ids == iota((POOL, 128), 1)).astype(F32)
    earlier = (iota((POOL, POOL), 1) < iota((POOL, POOL), 0)).astype(BF16)
    before = dot(earlier, onehot.astype(BF16))
    slot_rank = jnp.sum(onehot * before, axis=1, keepdims=True)
    slot = owner_ids.astype(F32) * float(PAD) + slot_rank
    for h in range(2):
        place[h] = (iota((POOL, SLOTS), 1).astype(F32) == slot + 8.0 * h).astype(BF16)

    loads["cot"].wait()
    left = dot_tn(spread[0], cot[:, 0:256]) + dot_tn(spread[1], cot[:, 256:512])
    out_buf[...] = left.astype(BF16)

    def normalize(i):
        width = ENCODERS[i][0]
        own = normed[i].at[0]
        loads[f"in{i}"].wait()
        for start, size in tiles_of(width, 384):
            block = own[:, start:start + size]
            own[:, start:start + size] = dot(perm[...], block).astype(BF16)
        gain = gains[i][...].reshape(1, width)

        def part(k, carry):
            rows = pl.ds(pl.multiple_of(k * 32, 32), 32)
            total = jnp.zeros((32, width), F32)
            for q in range(4):
                cells = pl.ds(pl.multiple_of(q * POOL + k * 32, 32), 32)
                values = own[cells, :].astype(F32)
                total = total + values
                mean = jnp.mean(values, axis=1, keepdims=True)
                centered = values - mean
                var = jnp.mean(centered * centered, axis=1, keepdims=True)
                own[cells, :] = (centered * lax.rsqrt(var + EPSILON) * gain).astype(BF16)
            bpart[rows, OFFSETS[i]:OFFSETS[i] + width] = (total * 0.0625).astype(BF16)
            return carry

        lax.fori_loop(0, POOL // 32, part, 0)

    half = pl.ds(pl.multiple_of(core * 192, 192), 192)
    plane_a = pl.ds(pl.multiple_of(core * 192, 96), POOL)
    plane_b = pl.ds(pl.multiple_of(core * 192 + POOL, 96), POOL)

    def rows_copy(i, k):
        axis = ENCODERS[i][3]
        src = (0, 0, 2, 1)[k]
        dst = (2, 1, 3, 3)[k]
        part = (half, half, plane_a, plane_b)[k]
        device = step_to(axis, 1 if k % 2 == 0 else 3)
        return remote(normed[i].at[src, part], normed[i].at[dst, part],
                      rows_send.at[i, k], rows_recv.at[i, k], device)

    def start(copy):
        copy.start()
        sends.append(copy)

    def sibling_rows(i, k):
        block = normed[i].at[(2, 1, 3)[k], half]
        start(remote(block, block, sibs_send.at[i, k], sibs_recv.at[i, k], sibling))

    def rows_start(i):
        for k in range(2):
            start(rows_copy(i, k))

    def rows_relay(i):
        for k in range(2):
            rows_copy(i, k).wait_recv()
            start(rows_copy(i, 2 + k))
            sibling_rows(i, k)

    def rows_last(i):
        for k in range(2, 4):
            rows_copy(i, k).wait_recv()
        sibling_rows(i, 2)

    other_half = pl.ds(pl.multiple_of((1 - core) * 192, 192), 192)

    def rows_wait(i, k):
        block = normed[i].at[(2, 1, 3)[k], other_half]
        remote(block, block, sibs_send.at[i, k], sibs_recv.at[i, k], sibling).wait_recv()

    def forward(i, first, count):
        width, hidden, _, _ = ENCODERS[i]
        rows = normed[i][first:first + count].reshape(count * ROWS, width)
        for start_at, size in tiles_of(hidden, TILE):
            cols = slice(start_at, start_at + size)
            if FLIPPED[i]:
                pre = dot_nt(rows, up[i][cols, :])
            else:
                pre = dot(rows, up[i][:, cols])
            cubic = 0.035677408136300125 * (pre * pre)
            linear = cubic + 0.7978845608028654
            tanh = jnp.tanh(pre * linear)
            upper = 0.5 + 0.5 * tanh
            act = pre * upper
            grad = upper + act * (1.0 - tanh) * (linear + (cubic + cubic))
            slope[i][first:first + count, :, cols] = grad.astype(BF16).reshape(count, ROWS, size)
            for s in range(count):
                cell = [act[s * ROWS + q * POOL:s * ROWS + (q + 1) * POOL] for q in range(4)]
                total = (cell[0] + cell[1]) + (cell[2] + cell[3])
                pact[i][(first + s) * POOL:(first + s + 1) * POOL, cols] = total.astype(BF16)

    def branch(i):
        width = ENCODERS[i][0]
        for start, size in tiles_of(width, 384):
            cols = slice(OFFSETS[i] + start, OFFSETS[i] + start + size)
            value = dot(pact[i][0:POOL, :], down[i][:, start:start + size]) * 0.25
            bpart[:, cols] = (bpart[:, cols].astype(F32) + value).astype(BF16)

    mine = pl.ds(pl.multiple_of(core * 48, 48), 48)
    theirs = pl.ds(pl.multiple_of(48 - core * 48, 48), 48)

    def sum_start(n, part, near):
        send(part.at[theirs], near, sum_send.at[n, 0], sum_recv.at[n, 0], sibling)

    def sum_cross(n, part, near, distant):
        remote(part.at[theirs], near, sum_send.at[n, 0], sum_recv.at[n, 0], sibling).wait_recv()
        part[mine, :] = (part[mine, :].astype(F32) + near[...].astype(F32)).astype(BF16)
        send(part.at[mine], distant, sum_send.at[n, 1], sum_recv.at[n, 1], far)

    def sum_wait(n, part, distant):
        remote(part.at[mine], distant, sum_send.at[n, 1], sum_recv.at[n, 1], far).wait_recv()

    def gfeat_finish(which):
        for i in which:
            width = ENCODERS[i][0]
            cols = slice(OFFSETS[i], OFFSETS[i] + width)
            total = gpart[mine, cols].astype(F32) + gpart_far[:, cols].astype(F32)
            gfeat[i][mine, :] = total.astype(BF16)
            for k in (1, 3, 2):
                start(gfeat_copy(i, k))
            start(gfeat_sibling(i, 0))

    def gfeat_copy(i, k):
        src = gfeat[i].at[mine]
        rows = pl.ds(pl.multiple_of(FROM[k] * POOL + core * 48, 48), 48)
        return remote(src, gfeat[i].at[rows], gf_send.at[i, k], gf_recv.at[i, k],
                      step_to(ENCODERS[i][3], k))

    def gfeat_sibling(i, k, arriving=False):
        at = (48 - core * 48) if arriving else core * 48
        block = gfeat[i].at[pl.ds(pl.multiple_of(FROM[k] * POOL + at, 48), 48)]
        return remote(block, block, gfs_send.at[i, k], gfs_recv.at[i, k], sibling)

    def gfeat_relay(i):
        for k in (1, 3, 2):
            gfeat_copy(i, k).wait_recv()
            start(gfeat_sibling(i, k))

    def gfeat_wait(i):
        for k in range(4):
            gfeat_sibling(i, k, True).wait_recv()

    def concat_finish():
        sum_wait(1, bpart, bpart_far)
        total = bpart[mine, :].astype(F32) + bpart_far[...].astype(F32)
        concat[mine, :] = total.astype(BF16)
        block = concat.at[mine]
        send(block, block, sum_send.at[1, 2], sum_recv.at[1, 2], sibling)

    def concat_wait():
        block = concat.at[theirs]
        remote(block, block, sum_send.at[1, 2], sum_recv.at[1, 2], sibling).wait_recv()

    def exchange(dst, send_sem, recv_sem):
        def one(k, carry):
            other = lax.rem(dp + k, N_DP)
            src = out_buf.at[pl.ds(pl.multiple_of(other * PAD, PAD), PAD)]
            to = dst.at[pl.ds(pl.multiple_of(dp * PAD, PAD), PAD)]
            device = {"enc": enc, "dp": other}
            remote(src, to, send_sem.at[k], recv_sem.at[k], device).start()
            return carry

        lax.fori_loop(1, N_DP, one, 0)
        here = pl.ds(pl.multiple_of(dp * PAD, PAD), PAD)
        dst[here, :] = out_buf[here, :]

    def exchange_wait(dst, send_sem, recv_sem, arrived):
        def one(k, carry):
            other = lax.rem(dp + k, N_DP) if not arrived else lax.rem(dp + N_DP - k, N_DP)
            src = out_buf.at[pl.ds(pl.multiple_of(other * PAD, PAD), PAD)]
            to = dst.at[pl.ds(pl.multiple_of(other * PAD, PAD), PAD)]
            device = {"enc": enc, "dp": other}
            copy = remote(src, to, send_sem.at[k], recv_sem.at[k], device)
            if arrived:
                copy.wait_recv()
            else:
                copy.wait_send()
            return carry

        lax.fori_loop(1, N_DP, one, 0)

    hold = up + (proj,)
    gpicked = perm
    ring = ("y", "z", "y", "z")

    def choice(rows_out, chunks, first):
        lanes_in = 384 if chunks == 0 else 256
        pieces = []
        for b in range(2 if chunks == 0 else chunks):
            r = iota((PICK, lanes_in), 0)
            at = r + first + b * (192 if chunks == 0 else rows_out)
            pieces.append(((iota((PICK, lanes_in), 1) == at) & (r < rows_out)).astype(BF16))
        return jnp.concatenate(pieces, axis=0)

    def backward(i, after):
        width, hidden, rows_out, axis = ENCODERS[i]
        p = position[axis]
        if axis == "y":
            choose[0:2 * PICK, 0:384] = choice(rows_out, 0, p * rows_out)
            for w in range(4):
                rows = slice(w * 2 * PICK, (w + 1) * 2 * PICK)
                cols = slice(w * 384, (w + 1) * 384)
                window = normed[i][:, :, cols].reshape(4 * ROWS, 384)
                picked[rows, :] = dot_nt(choose[0:2 * PICK, 0:384], window).astype(BF16)
                gpicked[rows, :] = dot_nt(choose[0:2 * PICK, 0:384], gfeat[i][:, cols]).astype(BF16)
        else:
            for xx in range(2):
                first = xx * 16 * rows_out + p * 4 * rows_out
                tile = lax.div(first, 128)
                choose[:, 0:256] = choice(rows_out, 4, first - tile * 128)
                rows = slice(xx * 4 * PICK, (xx + 1) * 4 * PICK)
                cols = pl.ds(pl.multiple_of(tile * 128, 128), 256)
                window = normed[i][:, :, cols].reshape(4 * ROWS, 256)
                picked[rows, :] = dot_nt(choose[:, 0:256], window).astype(BF16)
                gpicked[rows, :] = dot_nt(choose[:, 0:256], gfeat[i][:, cols]).astype(BF16)
        for start_at, size in tiles_of(hidden, TILE):
            cols = slice(start_at, start_at + size)
            grad_act = dot_nt(gfeat[i][...], down[i][cols, :])
            for s in range(4):
                grad = grad_act[s * POOL:(s + 1) * POOL]
                for q in range(4):
                    cells = slice(q * POOL, (q + 1) * POOL)
                    value = slope[i][s, cells, cols].astype(F32) * grad
                    slope[i][s, cells, cols] = value.astype(BF16)
            upper = dot(picked[...], slope[i][:, :, cols].reshape(4 * ROWS, size))
            lower = dot(gpicked[...], pact[i][:, cols])
            part = PARTS[i]
            for k in range(8):
                at = (k % 2) * 4 * PICK + (k // 2) * PICK
                rows = slice(at, at + part)
                both = jnp.concatenate([upper[rows], lower[rows]], axis=0).astype(BF16)
                hold[i][2 * k * part:2 * (k + 1) * part, cols] = both
            for action in after.get(start_at + size, ()):
                action()

    def chunk(n, b, xx):
        size = CHUNKS[n]
        return pl.ds(pl.multiple_of((b * 2 + xx) * size, size), size)

    def lanes_of(u):
        return pl.ds(UNITS[u][1], UNITS[u][2])

    def ring_copy(u, k):
        n = UNITS[u][0]
        axis = ring[n]
        p = position[axis]
        nxt, opp, prv = lax.rem(p + 1, 4), lax.rem(p + 2, 4), lax.rem(p + 3, 4)
        where = ((opp, 0), (opp, 1), (nxt, 1), (prv, 0), (nxt, 0), (prv, 1))[k]
        device = step_to(axis, 1 if k in (0, 2, 4) else 3)
        src = hold[n].at[chunk(n, *where), lanes_of(u)]
        return remote(src, land[u].at[k], rs_send.at[u, k], rs_recv.at[u, k], device)

    def reduce_start(u):
        for k in range(4):
            start(ring_copy(u, k))

    def reduce_mid(u):
        n = UNITS[u][0]
        p = position[ring[n]]
        for k, b, xx in ((0, lax.rem(p + 1, 4), 0), (1, lax.rem(p + 3, 4), 1)):
            ring_copy(u, k).wait_recv()
            rows = chunk(n, b, xx)
            total = hold[n][rows, lanes_of(u)].astype(F32) + land[u][k].astype(F32)
            hold[n][rows, lanes_of(u)] = total.astype(BF16)
            start(ring_copy(u, 4 + k))

    def cross_copy(u):
        n = UNITS[u][0]
        src = hold[n].at[chunk(n, position[ring[n]], 1 - x), lanes_of(u)]
        return remote(src, cross[u], x_send.at[u], x_recv.at[u], mirror)

    def ring_total(u, xx):
        n = UNITS[u][0]
        value = hold[n][chunk(n, position[ring[n]], xx), lanes_of(u)].astype(F32)
        return value + land[u][3 - xx].astype(F32) + land[u][4 + xx].astype(F32)

    def reduce_cross(u):
        n = UNITS[u][0]
        for k in range(2, 6):
            ring_copy(u, k).wait_recv()
        total = ring_total(u, 1 - x).astype(BF16)
        hold[n][chunk(n, position[ring[n]], 1 - x), lanes_of(u)] = total
        start(cross_copy(u))

    def reduce_end(u):
        n, first, _ = UNITS[u]
        cross_copy(u).wait_recv()
        total = ring_total(u, x) + cross[u][...].astype(F32)
        for k, out in enumerate(grads[n]):
            rows, width = out.shape
            last = min(first + UNITS[u][2], width)
            at = k * CHUNKS[n] // 2
            out[:, first:last] = total[at:at + rows, 0:last - first]

    def columns(a):
        def one(j, out):
            k = core * 4 + j
            index = lax.rem(k, 2) * 16 + lax.div(k, 2) * 4 + a
            r = iota((PROJ_CHUNK, 256), 0)
            hit = (iota((PROJ_CHUNK, 256), 1) == r + index * 4) & (r < 132)
            window = concat[:, pl.ds(pl.multiple_of(index * 128, 128), 256)]
            return dot_nt(hit.astype(BF16), window).astype(BF16)

        return one

    col_half = pl.ds(pl.multiple_of(core * 576, 576), 576)
    col_other = pl.ds(pl.multiple_of(576 - core * 576, 576), 576)

    def lane(pos):
        return slice(pos * 128, (pos + 1) * 128)

    def columns_start():
        for k in range(1, 4):
            one = columns(lax.rem(y + k, 4))

            def fill(j, carry, k=k, one=one):
                rows = pl.ds(pl.multiple_of(j * PROJ_CHUNK, PROJ_CHUNK), PROJ_CHUNK)
                cols_out[k - 1, rows, :] = one(j, None)
                return carry

            lax.fori_loop(0, 4, fill, 0)
            send(cols_out.at[k - 1], cols_in.at[col_half, lane(FROM[k])], cols_send.at[k],
                 cols_recv.at[k], step_to("y", k))
        one = columns(y)

        def fill_own(j, carry):
            rows = pl.ds(pl.multiple_of((core * 4 + j) * PROJ_CHUNK, PROJ_CHUNK), PROJ_CHUNK)
            cols_in[rows, lane(0)] = one(j, None)
            return carry

        lax.fori_loop(0, 4, fill_own, 0)
        block = cols_in.at[col_half, lane(0)]
        send(block, block, colf_send.at[0], colf_recv.at[0], sibling)

    def columns_relay():
        for k in range(1, 4):
            block = cols_in.at[col_half, lane(FROM[k])]
            remote(cols_out.at[k - 1], block, cols_send.at[k], cols_recv.at[k],
                   step_to("y", k)).wait_recv()
            send(block, block, colf_send.at[k], colf_recv.at[k], sibling)

    def columns_wait():
        for k in range(4):
            block = cols_in.at[col_other, lane(FROM[k])]
            remote(block, block, colf_send.at[k], colf_recv.at[k], sibling).wait_recv()

    def token_rows(pos):
        return tok_grads.at[pl.ds(pos * 128, 128)]

    def tokens_copy(k):
        return remote(token_rows(0), token_rows(FROM[k]), gt_send.at[k], gt_recv.at[k],
                      step_to("y", k))

    normalize(CNX)
    pl.semaphore_wait(barrier, N_DP + 1)
    exchange(cot_in, a2a_send, a2a_recv)
    rows_start(CNX)
    normalize(PIX)
    rows_start(PIX)
    normalize(SIG)

    loads["proj"].wait()
    exchange_wait(cot_in, a2a_send, a2a_recv, True)
    own_grads = jnp.concatenate(
        [dot(place[0], cot_in[...]), dot(place[1], cot_in[...])], axis=1
    ).astype(BF16)
    tok_grads[0:128, :] = jnp.concatenate([own_grads, jnp.zeros((32, LLM), BF16)], axis=0)
    for k in range(1, 4):
        start(tokens_copy(k))
    for start_at, size in tiles_of(CAT, 384):
        cols = slice(start_at, start_at + size)
        gpart[:, cols] = (dot_nt(tok_grads[0:POOL, :], proj[cols, :]) * 0.25).astype(BF16)
    sum_start(0, gpart, gpart_sib)

    loads[f"up{CNX}"].wait()
    forward(CNX, 0, 1)
    sum_cross(0, gpart, gpart_sib, gpart_far)
    loads[f"up{PIX}"].wait()
    forward(PIX, 0, 1)
    loads[f"up{SIG}"].wait()
    forward(SIG, 0, 1)
    for i in (CNX, PIX, SIG):
        loads[f"down{i}"].wait()
        branch(i)
    sum_start(1, bpart, bpart_sib)
    rows_relay(CNX)
    rows_relay(PIX)
    sum_cross(1, bpart, bpart_sib, bpart_far)
    sum_wait(0, gpart, gpart_far)
    gfeat_finish((CNX, PIX))
    concat[POOL:128, :] = jnp.zeros((32, CAT), BF16)

    rows_wait(CNX, 0)
    rows_wait(CNX, 1)
    forward(CNX, 1, 2)
    rows_start(SIG)
    gfeat_finish((SIG,))
    rows_last(CNX)
    rows_wait(PIX, 0)
    rows_wait(PIX, 1)
    forward(PIX, 1, 2)
    rows_last(PIX)
    rows_wait(CNX, 2)
    forward(CNX, 3, 1)
    concat_finish()
    gfeat_relay(CNX)
    rows_wait(PIX, 2)
    forward(PIX, 3, 1)
    concat_wait()

    exchange_wait(cot_in, a2a_send, a2a_recv, False)
    tokens = jnp.zeros((POOL, LLM), F32)
    for start_at, size in tiles_of(CAT, 384):
        cols = slice(start_at, start_at + size)
        tokens = tokens + dot(concat[0:POOL, cols], proj[cols, :])
    tokens = tokens.astype(BF16)
    left = dot_tn(place[0], tokens[:, 0:256]) + dot_tn(place[1], tokens[:, 256:512])
    out_buf[...] = left.astype(BF16)
    exchange(tok_in, a2b_send, a2b_recv)
    columns_start()
    gfeat_relay(PIX)

    def do(action, *args):
        return functools.partial(action, *args)

    gfeat_wait(CNX)
    backward(CNX, {768: (do(reduce_start, CNX_A),)})
    columns_relay()
    gfeat_wait(PIX)
    backward(PIX, {
        512: (do(reduce_start, PIX_A), do(rows_relay, SIG), do(reduce_mid, CNX_A)),
        992: (do(reduce_start, PIX_B),),
    })
    for k in range(1, 4):
        tokens_copy(k).wait_recv()
    columns_wait()
    for k in range(8):
        rows = slice(k * PROJ_CHUNK, (k + 1) * PROJ_CHUNK)
        proj[rows, :] = dot(cols_in[rows, :], tok_grads[...]).astype(BF16)
    reduce_start(PROJ_A)
    reduce_mid(PIX_A)
    gfeat_relay(SIG)
    rows_wait(SIG, 0)
    rows_wait(SIG, 1)
    forward(SIG, 1, 2)
    rows_last(SIG)
    reduce_mid(PIX_B)
    reduce_cross(CNX_A)
    exchange_wait(tok_in, a2b_send, a2b_recv, True)
    projected[:, 0:256] = dot(spread[0], tok_in[...]).astype(BF16)
    projected[:, 256:512] = dot(spread[1], tok_in[...]).astype(BF16)
    rows_wait(SIG, 2)
    forward(SIG, 3, 1)
    reduce_mid(PROJ_A)
    gfeat_wait(SIG)
    backward(SIG, {
        512: (do(reduce_start, SIG_A), do(reduce_cross, PIX_A), do(reduce_end, CNX_A)),
        1076: (do(reduce_start, SIG_B),),
    })
    reduce_mid(SIG_A)
    reduce_cross(PROJ_A)
    reduce_cross(PIX_B)
    reduce_end(PIX_A)
    reduce_mid(SIG_B)
    reduce_end(PROJ_A)
    reduce_end(PIX_B)
    reduce_cross(SIG_A)
    reduce_cross(SIG_B)
    reduce_end(SIG_A)
    reduce_end(SIG_B)

    exchange_wait(tok_in, a2b_send, a2b_recv, False)
    for copy in sends:
        copy.wait_send()


def hand_over(*refs):
    for k in range(8):
        refs[8 + k][...] = refs[k][...]


def local(
    sig_in, sig_gain, sig_up, sig_down, cnx_in, cnx_gain, cnx_up, cnx_down,
    pix_in, pix_gain, pix_up, pix_down, proj_weight, owners, cotangent,
):
    any_spec = pl.BlockSpec(memory_space=pl.ANY)
    vmem_spec = pl.BlockSpec(memory_space=pltpu.VMEM)
    vmem = pltpu.VMEM
    dma = pltpu.SemaphoreType.DMA
    widths = [e[0] for e in ENCODERS]
    hiddens = [e[1] for e in ENCODERS]
    scratch = (
        [vmem((4, ROWS, w), BF16) for w in widths]
        + [vmem((4, ROWS, h), BF16) for h in hiddens]
        + [vmem((4 * POOL, h), BF16) for h in hiddens]
        + [vmem((h, w) if f else (w, h), BF16) for w, h, f in zip(widths, hiddens, FLIPPED)]
        + [vmem((h, w), BF16) for w, h in zip(widths, hiddens)]
        + [vmem((4 * POOL, w), BF16) for w in widths]
        + [vmem((6, CHUNKS[n], w), BF16) for n, _, w in UNITS]
        + [vmem((CHUNKS[n], w), BF16) for n, _, w in UNITS]
        + [
            vmem((CAT, LLM), BF16),
            vmem((N_DP * CAP, LLM), BF16),
            vmem((2, N_DP * CAP, SLOTS), BF16),
            vmem((ROWS, ROWS), BF16),
            vmem((2, POOL, SLOTS), BF16),
            vmem((SLOTS, LLM // 2), BF16),
            vmem((SLOTS, LLM // 2), BF16),
            vmem((SLOTS, LLM // 2), BF16),
            vmem((512, LLM), BF16),
            vmem((POOL, CAT), BF16),
            vmem((POOL // 2, CAT), BF16),
            vmem((POOL // 2, CAT), BF16),
            vmem((POOL, CAT), BF16),
            vmem((POOL // 2, CAT), BF16),
            vmem((POOL // 2, CAT), BF16),
            vmem((128, CAT), BF16),
            vmem((3, 4 * PROJ_CHUNK, 128), BF16),
            vmem((8 * PROJ_CHUNK, LLM), BF16),
            vmem((4 * PICK, 384), BF16),
            vmem((8 * PICK, 4 * ROWS), BF16),
        ]
        + [
            dma((11,)),
            dma((N_DP,)), dma((N_DP,)), dma((N_DP,)), dma((N_DP,)),
            dma((4,)), dma((4,)), dma((4,)), dma((4,)), dma((4,)), dma((4,)),
            dma((3, 4)), dma((3, 4)), dma((3, 3)), dma((3, 3)),
            dma((2, 3)), dma((2, 3)),
            dma((3, 4)), dma((3, 4)), dma((3, 4)), dma((3, 4)),
            dma((6, 6)), dma((6, 6)), dma((6,)), dma((6,)),
        ]
    )
    outs = pl.pallas_call(
        kernel,
        out_shape=[
            jax.ShapeDtypeStruct((N_DP * CAP, LLM), BF16),
            *[jax.ShapeDtypeStruct((e[2], e[1]), F32) for e in ENCODERS for _ in range(2)],
            jax.ShapeDtypeStruct((132, LLM), F32),
        ],
        in_specs=[any_spec] * 11 + [vmem_spec] * 4,
        out_specs=[vmem_spec] * 8,
        scratch_shapes=scratch,
        compiler_params=pltpu.CompilerParams(
            collective_id=0, has_side_effects=True, vmem_limit_bytes=64 * 2**20
        ),
        cost_estimate=pl.CostEstimate(flops=2 * 10**10, bytes_accessed=3 * 10**7, transcendentals=0),
    )(
        sig_in, cnx_in, pix_in, sig_up.T, cnx_up, pix_up.T, sig_down, cnx_down, pix_down,
        proj_weight, cotangent, owners.T,
        sig_gain, cnx_gain, pix_gain,
    )
    outs = pl.pallas_call(
        hand_over,
        out_shape=[jax.ShapeDtypeStruct(o.shape, o.dtype) for o in outs],
        in_specs=[vmem_spec] * 8,
        out_specs=[vmem_spec] * 8,
    )(*outs)
    return (outs[0][None], outs[1], outs[2].T, outs[3], outs[4].T, outs[5], outs[6].T, outs[7])


def solution(mesh):
    placed = (
        P("dp", None), P(), P(None, "enc"), P("enc", None),
        P("dp", None), P(), P(None, "enc"), P("enc", None),
        P("dp", None), P(), P(None, "enc"), P("enc", None),
        P(None, "enc"), P("dp", None), P("dp", None, "enc"),
    )
    return jax.shard_map(
        local,
        mesh=mesh,
        in_specs=placed,
        out_specs=(
            P("dp", None, "enc"), P("dp", "enc"), P("enc", "dp"), P("dp", "enc"),
            P("enc", "dp"), P("dp", "enc"), P("enc", "dp"), P("dp", "enc"),
        ),
        check_vma=False,
    )
```

```python
import functools

import jax
import jax.numpy as jnp
from jax import lax
from jax.experimental import pallas as pl
from jax.experimental.pallas import tpu as pltpu
from jax.sharding import PartitionSpec as P

F32 = jnp.float32
BF16 = jnp.bfloat16
MESH = pl.DeviceIdType.MESH
EPSILON = 1e-06
GRID = 64
ROWS = 384
POOL = 96
CAT = 4224
LLM = 512
CAP = 6
PAD = 16
N_DP = 32
SLOTS = N_DP * PAD
PICK = 48
PROJ_CHUNK = 144
TILE = 256

ENCODERS = ((1152, 1076, 36, "z"), (1536, 768, 48, "y"), (1536, 992, 48, "z"))
OFFSETS = (0, 1152, 2688)
PARTS = (40, 48, 48)
CHUNKS = (80, 96, 96, PROJ_CHUNK)
UNITS = ((0, 0, 512), (0, 512, 640), (1, 0, 768), (2, 0, 512), (2, 512, 512), (3, 0, LLM))
SIG_A, SIG_B, CNX_A, PIX_A, PIX_B, PROJ_A = range(6)
FROM = (0, 2, 3, 1)
FLIPPED = (True, False, True)
SIG, CNX, PIX = 0, 1, 2


def dot(left, right):
    return jnp.dot(left, right, preferred_element_type=F32)


def dot_nt(left, right):
    return lax.dot_general(left, right, (((1,), (1,)), ((), ())), preferred_element_type=F32)


def dot_tn(left, right):
    return lax.dot_general(left, right, (((0,), (0,)), ((), ())), preferred_element_type=F32)


def iota(shape, axis):
    return lax.broadcasted_iota(jnp.int32, shape, axis)


def tiles_of(extent, width):
    return [(start, min(width, extent - start)) for start in range(0, extent, width)]


def kernel(*refs):
    ins = refs[0:3]
    ups_hbm = refs[3:6]
    downs_hbm = refs[6:9]
    proj_hbm, cot_hbm, owners, *gains = refs[9:15]
    projected = refs[15]
    grads = ((refs[16], refs[17]), (refs[18], refs[19]), (refs[20], refs[21]), (refs[22],))
    (
        normed_0, normed_1, normed_2, slope_0, slope_1, slope_2, pact_0, pact_1, pact_2,
        up_0, up_1, up_2, down_0, down_1, down_2, gfeat_0, gfeat_1, gfeat_2,
        land_0, land_1, land_2, land_3, land_4, land_5,
        cross_0, cross_1, cross_2, cross_3, cross_4, cross_5,
        proj, cot, spread, perm, place, out_buf, cot_in, tok_in, tok_grads,
        gpart, gpart_sib, gpart_far, bpart, bpart_sib, bpart_far, concat,
        cols_out, cols_in, choose, picked,
        load_sem, a2a_send, a2a_recv, a2b_send, a2b_recv, gt_send, gt_recv, cols_send, cols_recv,
        colf_send, colf_recv, rows_send, rows_recv, sibs_send, sibs_recv, sum_send, sum_recv,
        gf_send, gf_recv, gfs_send, gfs_recv, rs_send, rs_recv, x_send, x_recv,
    ) = refs[23:]
    normed = (normed_0, normed_1, normed_2)
    slope = (slope_0, slope_1, slope_2)
    pact = (pact_0, pact_1, pact_2)
    up = (up_0, up_1, up_2)
    down = (down_0, down_1, down_2)
    gfeat = (gfeat_0, gfeat_1, gfeat_2)
    land = (land_0, land_1, land_2, land_3, land_4, land_5)
    cross = (cross_0, cross_1, cross_2, cross_3, cross_4, cross_5)

    enc = lax.axis_index("enc")
    dp = lax.axis_index("dp")
    core = lax.rem(enc, 2)
    x = lax.div(dp, 16)
    z = lax.rem(lax.div(dp, 4), 4)
    y = lax.rem(dp, 4)
    sibling = {"enc": enc + 1 - 2 * core, "dp": dp}
    far = {"enc": lax.rem(enc + 2, 4), "dp": dp}
    mirror = {"enc": enc, "dp": (1 - x) * 16 + z * 4 + y}
    position = {"z": z, "y": y}

    def step_to(axis, k):
        if axis == "z":
            return {"enc": enc, "dp": x * 16 + lax.rem(z + k, 4) * 4 + y}
        return {"enc": enc, "dp": x * 16 + z * 4 + lax.rem(y + k, 4)}

    sends = []

    def remote(src, dst, send, recv, device):
        return pltpu.make_async_remote_copy(
            src_ref=src, dst_ref=dst, send_sem=send, recv_sem=recv, device_id=device,
            device_id_type=MESH,
        )

    def send(src, dst, send_sem, recv_sem, device):
        copy = remote(src, dst, send_sem, recv_sem, device)
        copy.start()
        sends.append(copy)
        return copy

    barrier = pltpu.get_barrier_semaphore()

    def greet(k, carry):
        other = {"enc": enc, "dp": lax.rem(dp + k, N_DP)}
        pl.semaphore_signal(barrier, inc=1, device_id=other, device_id_type=MESH)
        return carry

    lax.fori_loop(1, N_DP, greet, 0)
    for other in (sibling, far):
        pl.semaphore_signal(barrier, inc=1, device_id=other, device_id_type=MESH)

    loads = {}

    def load(name, src, dst):
        copy = pltpu.make_async_copy(src, dst, load_sem.at[len(loads)])
        copy.start()
        loads[name] = copy

    load("cot", cot_hbm.at[0], cot)
    for i in (CNX, PIX, SIG):
        load(f"in{i}", ins[i], normed[i].at[0])
    load("proj", proj_hbm, proj)
    for i in (CNX, PIX, SIG):
        load(f"up{i}", ups_hbm[i], up[i])
    for i in (CNX, PIX, SIG):
        load(f"down{i}", downs_hbm[i], down[i])

    for q in range(4):
        pooled = iota((POOL, ROWS), 0)
        origin = lax.shift_right_logical(pooled, 5) * 128 + (q // 2) * 64
        origin = origin + lax.bitwise_and(pooled, 31) * 2 + q % 2
        perm[q * POOL:(q + 1) * POOL, :] = (iota((POOL, ROWS), 1) == origin).astype(BF16)

    wide = iota((N_DP * CAP, SLOTS), 1)
    for h in range(2):
        rank = lax.bitwise_and(wide, PAD - 1) - 8 * h
        target = lax.shift_right_logical(wide, 4) * CAP + rank
        hit = (iota((N_DP * CAP, SLOTS), 0) == target) & (rank >= 0) & (rank < CAP)
        spread[h] = hit.astype(BF16)

    diagonal = iota((POOL, POOL), 0) == iota((POOL, POOL), 1)
    owner_ids = jnp.sum(jnp.where(diagonal, owners[...], 0), axis=1, keepdims=True)
    onehot = (owner_ids == iota((POOL, 128), 1)).astype(F32)
    earlier = (iota((POOL, POOL), 1) < iota((POOL, POOL), 0)).astype(BF16)
    before = dot(earlier, onehot.astype(BF16))
    slot_rank = jnp.sum(onehot * before, axis=1, keepdims=True)
    slot = owner_ids.astype(F32) * float(PAD) + slot_rank
    for h in range(2):
        place[h] = (iota((POOL, SLOTS), 1).astype(F32) == slot + 8.0 * h).astype(BF16)

    loads["cot"].wait()
    left = dot_tn(spread[0], cot[:, 0:256]) + dot_tn(spread[1], cot[:, 256:512])
    out_buf[...] = left.astype(BF16)

    def normalize(i):
        width = ENCODERS[i][0]
        own = normed[i].at[0]
        loads[f"in{i}"].wait()
        for start, size in tiles_of(width, 384):
            block = own[:, start:start + size]
            own[:, start:start + size] = dot(perm[...], block).astype(BF16)
        gain = gains[i][...].reshape(1, width)

        def part(k, carry):
            rows = pl.ds(pl.multiple_of(k * 32, 32), 32)
            total = jnp.zeros((32, width), F32)
            for q in range(4):
                cells = pl.ds(pl.multiple_of(q * POOL + k * 32, 32), 32)
                values = own[cells, :].astype(F32)
                total = total + values
                mean = jnp.mean(values, axis=1, keepdims=True)
                centered = values - mean
                var = jnp.mean(centered * centered, axis=1, keepdims=True)
                own[cells, :] = (centered * lax.rsqrt(var + EPSILON) * gain).astype(BF16)
            bpart[rows, OFFSETS[i]:OFFSETS[i] + width] = (total * 0.0625).astype(BF16)
            return carry

        lax.fori_loop(0, POOL // 32, part, 0)

    half = pl.ds(pl.multiple_of(core * 192, 192), 192)
    plane_a = pl.ds(pl.multiple_of(core * 192, 96), POOL)
    plane_b = pl.ds(pl.multiple_of(core * 192 + POOL, 96), POOL)

    def rows_copy(i, k):
        axis = ENCODERS[i][3]
        src = (0, 0, 2, 1)[k]
        dst = (2, 1, 3, 3)[k]
        part = (half, half, plane_a, plane_b)[k]
        device = step_to(axis, 1 if k % 2 == 0 else 3)
        return remote(normed[i].at[src, part], normed[i].at[dst, part],
                      rows_send.at[i, k], rows_recv.at[i, k], device)

    def start(copy):
        copy.start()
        sends.append(copy)

    def sibling_rows(i, k):
        block = normed[i].at[(2, 1, 3)[k], half]
        start(remote(block, block, sibs_send.at[i, k], sibs_recv.at[i, k], sibling))

    def rows_start(i):
        for k in range(2):
            start(rows_copy(i, k))

    def rows_relay(i):
        for k in range(2):
            rows_copy(i, k).wait_recv()
            start(rows_copy(i, 2 + k))
            sibling_rows(i, k)

    def rows_last(i):
        for k in range(2, 4):
            rows_copy(i, k).wait_recv()
        sibling_rows(i, 2)

    other_half = pl.ds(pl.multiple_of((1 - core) * 192, 192), 192)

    def rows_wait(i, k):
        block = normed[i].at[(2, 1, 3)[k], other_half]
        remote(block, block, sibs_send.at[i, k], sibs_recv.at[i, k], sibling).wait_recv()

    def over_tiles(first, last, body):
        whole = last // TILE

        def one(t, carry):
            body(pl.ds(pl.multiple_of(t * TILE, TILE), TILE), TILE)
            return carry

        lax.fori_loop(first // TILE, whole, one, 0)
        if last > whole * TILE:
            body(slice(whole * TILE, last), last - whole * TILE)

    def forward(i, first, count):
        width, hidden, _, _ = ENCODERS[i]

        def tile(cols, size):
            rows = normed[i][first:first + count].reshape(count * ROWS, width)
            if FLIPPED[i]:
                pre = dot_nt(rows, up[i][cols, :])
            else:
                pre = dot(rows, up[i][:, cols])
            cubic = 0.035677408136300125 * (pre * pre)
            linear = cubic + 0.7978845608028654
            tanh = jnp.tanh(pre * linear)
            upper = 0.5 + 0.5 * tanh
            act = pre * upper
            grad = upper + act * (1.0 - tanh) * (linear + (cubic + cubic))
            slope[i][first:first + count, :, cols] = grad.astype(BF16).reshape(count, ROWS, size)
            for s in range(count):
                cell = [act[s * ROWS + q * POOL:s * ROWS + (q + 1) * POOL] for q in range(4)]
                total = (cell[0] + cell[1]) + (cell[2] + cell[3])
                pact[i][(first + s) * POOL:(first + s + 1) * POOL, cols] = total.astype(BF16)

        for start_at, size in tiles_of(hidden, TILE):
            tile(slice(start_at, start_at + size), size)

    def branch(i):
        width = ENCODERS[i][0]
        for start, size in tiles_of(width, 384):
            cols = slice(OFFSETS[i] + start, OFFSETS[i] + start + size)
            value = dot(pact[i][0:POOL, :], down[i][:, start:start + size]) * 0.25
            bpart[:, cols] = (bpart[:, cols].astype(F32) + value).astype(BF16)

    mine = pl.ds(pl.multiple_of(core * 48, 48), 48)
    theirs = pl.ds(pl.multiple_of(48 - core * 48, 48), 48)

    def sum_start(n, part, near):
        send(part.at[theirs], near, sum_send.at[n, 0], sum_recv.at[n, 0], sibling)

    def sum_cross(n, part, near, distant):
        remote(part.at[theirs], near, sum_send.at[n, 0], sum_recv.at[n, 0], sibling).wait_recv()
        part[mine, :] = (part[mine, :].astype(F32) + near[...].astype(F32)).astype(BF16)
        send(part.at[mine], distant, sum_send.at[n, 1], sum_recv.at[n, 1], far)

    def sum_wait(n, part, distant):
        remote(part.at[mine], distant, sum_send.at[n, 1], sum_recv.at[n, 1], far).wait_recv()

    def gfeat_finish(which):
        for i in which:
            width = ENCODERS[i][0]
            cols = slice(OFFSETS[i], OFFSETS[i] + width)
            total = gpart[mine, cols].astype(F32) + gpart_far[:, cols].astype(F32)
            gfeat[i][mine, :] = total.astype(BF16)
            for k in (1, 3, 2):
                start(gfeat_copy(i, k))
            start(gfeat_sibling(i, 0))

    def gfeat_copy(i, k):
        src = gfeat[i].at[mine]
        rows = pl.ds(pl.multiple_of(FROM[k] * POOL + core * 48, 48), 48)
        return remote(src, gfeat[i].at[rows], gf_send.at[i, k], gf_recv.at[i, k],
                      step_to(ENCODERS[i][3], k))

    def gfeat_sibling(i, k, arriving=False):
        at = (48 - core * 48) if arriving else core * 48
        block = gfeat[i].at[pl.ds(pl.multiple_of(FROM[k] * POOL + at, 48), 48)]
        return remote(block, block, gfs_send.at[i, k], gfs_recv.at[i, k], sibling)

    def gfeat_relay(i):
        for k in (1, 3, 2):
            gfeat_copy(i, k).wait_recv()
            start(gfeat_sibling(i, k))

    def gfeat_wait(i):
        for k in range(4):
            gfeat_sibling(i, k, True).wait_recv()

    def concat_finish():
        sum_wait(1, bpart, bpart_far)
        total = bpart[mine, :].astype(F32) + bpart_far[...].astype(F32)
        concat[mine, :] = total.astype(BF16)
        block = concat.at[mine]
        send(block, block, sum_send.at[1, 2], sum_recv.at[1, 2], sibling)

    def concat_wait():
        block = concat.at[theirs]
        remote(block, block, sum_send.at[1, 2], sum_recv.at[1, 2], sibling).wait_recv()

    def exchange(dst, send_sem, recv_sem):
        def one(k, carry):
            other = lax.rem(dp + k, N_DP)
            src = out_buf.at[pl.ds(pl.multiple_of(other * PAD, PAD), PAD)]
            to = dst.at[pl.ds(pl.multiple_of(dp * PAD, PAD), PAD)]
            device = {"enc": enc, "dp": other}
            remote(src, to, send_sem.at[k], recv_sem.at[k], device).start()
            return carry

        lax.fori_loop(1, N_DP, one, 0)
        here = pl.ds(pl.multiple_of(dp * PAD, PAD), PAD)
        dst[here, :] = out_buf[here, :]

    def exchange_wait(dst, send_sem, recv_sem, arrived):
        def one(k, carry):
            other = lax.rem(dp + k, N_DP) if not arrived else lax.rem(dp + N_DP - k, N_DP)
            src = out_buf.at[pl.ds(pl.multiple_of(other * PAD, PAD), PAD)]
            to = dst.at[pl.ds(pl.multiple_of(other * PAD, PAD), PAD)]
            device = {"enc": enc, "dp": other}
            copy = remote(src, to, send_sem.at[k], recv_sem.at[k], device)
            if arrived:
                copy.wait_recv()
            else:
                copy.wait_send()
            return carry

        lax.fori_loop(1, N_DP, one, 0)

    hold = up + (proj,)
    gpicked = perm
    ring = ("y", "z", "y", "z")

    def choice(rows_out, chunks, first):
        lanes_in = 384 if chunks == 0 else 256
        pieces = []
        for b in range(2 if chunks == 0 else chunks):
            r = iota((PICK, lanes_in), 0)
            at = r + first + b * (192 if chunks == 0 else rows_out)
            pieces.append(((iota((PICK, lanes_in), 1) == at) & (r < rows_out)).astype(BF16))
        return jnp.concatenate(pieces, axis=0)

    def backward(i, after):
        width, hidden, rows_out, axis = ENCODERS[i]
        p = position[axis]
        if axis == "y":
            choose[0:2 * PICK, 0:384] = choice(rows_out, 0, p * rows_out)
            for w in range(4):
                rows = slice(w * 2 * PICK, (w + 1) * 2 * PICK)
                cols = slice(w * 384, (w + 1) * 384)
                window = normed[i][:, :, cols].reshape(4 * ROWS, 384)
                picked[rows, :] = dot_nt(choose[0:2 * PICK, 0:384], window).astype(BF16)
                gpicked[rows, :] = dot_nt(choose[0:2 * PICK, 0:384], gfeat[i][:, cols]).astype(BF16)
        else:
            for xx in range(2):
                first = xx * 16 * rows_out + p * 4 * rows_out
                tile = lax.div(first, 128)
                choose[:, 0:256] = choice(rows_out, 4, first - tile * 128)
                rows = slice(xx * 4 * PICK, (xx + 1) * 4 * PICK)
                cols = pl.ds(pl.multiple_of(tile * 128, 128), 256)
                window = normed[i][:, :, cols].reshape(4 * ROWS, 256)
                picked[rows, :] = dot_nt(choose[:, 0:256], window).astype(BF16)
                gpicked[rows, :] = dot_nt(choose[:, 0:256], gfeat[i][:, cols]).astype(BF16)
        def tile(cols, size):
            grad_act = dot_nt(gfeat[i][...], down[i][cols, :])
            for s in range(4):
                grad = grad_act[s * POOL:(s + 1) * POOL].astype(BF16)
                for q in range(4):
                    cells = slice(q * POOL, (q + 1) * POOL)
                    slope[i][s, cells, cols] = slope[i][s, cells, cols] * grad
            upper = dot(picked[...], slope[i][:, :, cols].reshape(4 * ROWS, size))
            lower = dot(gpicked[...], pact[i][:, cols])
            part = PARTS[i]
            for k in range(8):
                at = (k % 2) * 4 * PICK + (k // 2) * PICK
                rows = slice(at, at + part)
                both = jnp.concatenate([upper[rows], lower[rows]], axis=0).astype(BF16)
                hold[i][2 * k * part:2 * (k + 1) * part, cols] = both

        done = 0
        for last in sorted(after):
            over_tiles(done, last, tile)
            done = last
            for action in after[last]:
                action()

    def chunk(n, b, xx):
        size = CHUNKS[n]
        return pl.ds(pl.multiple_of((b * 2 + xx) * size, size), size)

    def lanes_of(u):
        return pl.ds(UNITS[u][1], UNITS[u][2])

    def ring_copy(u, k):
        n = UNITS[u][0]
        axis = ring[n]
        p = position[axis]
        nxt, opp, prv = lax.rem(p + 1, 4), lax.rem(p + 2, 4), lax.rem(p + 3, 4)
        where = ((opp, 0), (opp, 1), (nxt, 1), (prv, 0), (nxt, 0), (prv, 1))[k]
        device = step_to(axis, 1 if k in (0, 2, 4) else 3)
        src = hold[n].at[chunk(n, *where), lanes_of(u)]
        return remote(src, land[u].at[k], rs_send.at[u, k], rs_recv.at[u, k], device)

    def reduce_start(u):
        for k in range(4):
            start(ring_copy(u, k))

    def reduce_mid(u):
        n = UNITS[u][0]
        p = position[ring[n]]
        for k, b, xx in ((0, lax.rem(p + 1, 4), 0), (1, lax.rem(p + 3, 4), 1)):
            ring_copy(u, k).wait_recv()
            rows = chunk(n, b, xx)
            total = hold[n][rows, lanes_of(u)].astype(F32) + land[u][k].astype(F32)
            hold[n][rows, lanes_of(u)] = total.astype(BF16)
            start(ring_copy(u, 4 + k))

    def cross_copy(u):
        n = UNITS[u][0]
        src = hold[n].at[chunk(n, position[ring[n]], 1 - x), lanes_of(u)]
        return remote(src, cross[u], x_send.at[u], x_recv.at[u], mirror)

    def ring_total(u, xx):
        n = UNITS[u][0]
        value = hold[n][chunk(n, position[ring[n]], xx), lanes_of(u)].astype(F32)
        return value + land[u][3 - xx].astype(F32) + land[u][4 + xx].astype(F32)

    def reduce_cross(u):
        n = UNITS[u][0]
        for k in range(2, 6):
            ring_copy(u, k).wait_recv()
        total = ring_total(u, 1 - x).astype(BF16)
        hold[n][chunk(n, position[ring[n]], 1 - x), lanes_of(u)] = total
        start(cross_copy(u))

    def reduce_end(u):
        n, first, _ = UNITS[u]
        cross_copy(u).wait_recv()
        total = ring_total(u, x) + cross[u][...].astype(F32)
        for k, out in enumerate(grads[n]):
            rows, width = out.shape
            last = min(first + UNITS[u][2], width)
            at = k * CHUNKS[n] // 2
            out[:, first:last] = total[at:at + rows, 0:last - first]

    def columns(a):
        def one(j, out):
            k = core * 4 + j
            index = lax.rem(k, 2) * 16 + lax.div(k, 2) * 4 + a
            r = iota((PROJ_CHUNK, 256), 0)
            hit = (iota((PROJ_CHUNK, 256), 1) == r + index * 4) & (r < 132)
            window = concat[:, pl.ds(pl.multiple_of(index * 128, 128), 256)]
            return dot_nt(hit.astype(BF16), window).astype(BF16)

        return one

    col_half = pl.ds(pl.multiple_of(core * 576, 576), 576)
    col_other = pl.ds(pl.multiple_of(576 - core * 576, 576), 576)

    def lane(pos):
        return slice(pos * 128, (pos + 1) * 128)

    def columns_start():
        for k in range(1, 4):
            one = columns(lax.rem(y + k, 4))

            def fill(j, carry, k=k, one=one):
                rows = pl.ds(pl.multiple_of(j * PROJ_CHUNK, PROJ_CHUNK), PROJ_CHUNK)
                cols_out[k - 1, rows, :] = one(j, None)
                return carry

            lax.fori_loop(0, 4, fill, 0)
            send(cols_out.at[k - 1], cols_in.at[col_half, lane(FROM[k])], cols_send.at[k],
                 cols_recv.at[k], step_to("y", k))
        one = columns(y)

        def fill_own(j, carry):
            rows = pl.ds(pl.multiple_of((core * 4 + j) * PROJ_CHUNK, PROJ_CHUNK), PROJ_CHUNK)
            cols_in[rows, lane(0)] = one(j, None)
            return carry

        lax.fori_loop(0, 4, fill_own, 0)
        block = cols_in.at[col_half, lane(0)]
        send(block, block, colf_send.at[0], colf_recv.at[0], sibling)

    def columns_relay():
        for k in range(1, 4):
            block = cols_in.at[col_half, lane(FROM[k])]
            remote(cols_out.at[k - 1], block, cols_send.at[k], cols_recv.at[k],
                   step_to("y", k)).wait_recv()
            send(block, block, colf_send.at[k], colf_recv.at[k], sibling)

    def columns_wait():
        for k in range(4):
            block = cols_in.at[col_other, lane(FROM[k])]
            remote(block, block, colf_send.at[k], colf_recv.at[k], sibling).wait_recv()

    def token_rows(pos):
        return tok_grads.at[pl.ds(pos * 128, 128)]

    def tokens_copy(k):
        return remote(token_rows(0), token_rows(FROM[k]), gt_send.at[k], gt_recv.at[k],
                      step_to("y", k))

    normalize(CNX)
    pl.semaphore_wait(barrier, N_DP + 1)
    exchange(cot_in, a2a_send, a2a_recv)
    rows_start(CNX)
    normalize(PIX)
    rows_start(PIX)
    normalize(SIG)

    loads["proj"].wait()
    exchange_wait(cot_in, a2a_send, a2a_recv, True)
    own_grads = jnp.concatenate(
        [dot(place[0], cot_in[...]), dot(place[1], cot_in[...])], axis=1
    ).astype(BF16)
    tok_grads[0:128, :] = jnp.concatenate([own_grads, jnp.zeros((32, LLM), BF16)], axis=0)
    for k in range(1, 4):
        start(tokens_copy(k))
    for start_at, size in tiles_of(CAT, 384):
        cols = slice(start_at, start_at + size)
        gpart[:, cols] = (dot_nt(tok_grads[0:POOL, :], proj[cols, :]) * 0.25).astype(BF16)
    sum_start(0, gpart, gpart_sib)

    loads[f"up{CNX}"].wait()
    forward(CNX, 0, 1)
    sum_cross(0, gpart, gpart_sib, gpart_far)
    loads[f"up{PIX}"].wait()
    forward(PIX, 0, 1)
    loads[f"up{SIG}"].wait()
    forward(SIG, 0, 1)
    for i in (CNX, PIX, SIG):
        loads[f"down{i}"].wait()
        branch(i)
    sum_start(1, bpart, bpart_sib)
    rows_relay(CNX)
    rows_relay(PIX)
    sum_cross(1, bpart, bpart_sib, bpart_far)
    sum_wait(0, gpart, gpart_far)
    gfeat_finish((CNX, PIX))
    concat[POOL:128, :] = jnp.zeros((32, CAT), BF16)

    rows_wait(CNX, 0)
    rows_wait(CNX, 1)
    forward(CNX, 1, 2)
    rows_wait(PIX, 0)
    rows_wait(PIX, 1)
    rows_last(CNX)
    forward(PIX, 1, 2)
    rows_start(SIG)
    rows_wait(CNX, 2)
    forward(CNX, 3, 1)
    concat_finish()
    gfeat_finish((SIG,))
    concat_wait()

    exchange_wait(cot_in, a2a_send, a2a_recv, False)
    tokens = jnp.zeros((POOL, LLM), F32)
    for start_at, size in tiles_of(CAT, 384):
        cols = slice(start_at, start_at + size)
        tokens = tokens + dot(concat[0:POOL, cols], proj[cols, :])
    tokens = tokens.astype(BF16)
    left = dot_tn(place[0], tokens[:, 0:256]) + dot_tn(place[1], tokens[:, 256:512])
    out_buf[...] = left.astype(BF16)
    exchange(tok_in, a2b_send, a2b_recv)
    columns_start()
    gfeat_relay(CNX)
    rows_last(PIX)

    def do(action, *args):
        return functools.partial(action, *args)

    gfeat_wait(CNX)
    backward(CNX, {768: (do(reduce_start, CNX_A),)})
    gfeat_relay(PIX)
    rows_wait(PIX, 2)
    forward(PIX, 3, 1)
    columns_relay()
    gfeat_wait(PIX)
    backward(PIX, {
        512: (do(reduce_start, PIX_A), do(rows_relay, SIG), do(reduce_mid, CNX_A)),
        992: (do(reduce_start, PIX_B),),
    })
    for k in range(1, 4):
        tokens_copy(k).wait_recv()
    columns_wait()
    for k in range(8):
        rows = slice(k * PROJ_CHUNK, (k + 1) * PROJ_CHUNK)
        proj[rows, :] = dot(cols_in[rows, :], tok_grads[...]).astype(BF16)
    reduce_start(PROJ_A)
    reduce_mid(PIX_A)
    gfeat_relay(SIG)
    rows_wait(SIG, 0)
    rows_wait(SIG, 1)
    forward(SIG, 1, 2)
    rows_last(SIG)
    reduce_mid(PIX_B)
    rows_wait(SIG, 2)
    forward(SIG, 3, 1)
    reduce_mid(PROJ_A)
    gfeat_wait(SIG)
    backward(SIG, {
        512: (do(reduce_start, SIG_A), do(reduce_cross, CNX_A)),
        1076: (do(reduce_start, SIG_B),),
    })
    reduce_mid(SIG_A)
    reduce_cross(PIX_A)
    reduce_cross(PROJ_A)
    reduce_cross(PIX_B)
    reduce_mid(SIG_B)
    exchange_wait(tok_in, a2b_send, a2b_recv, True)
    projected[:, 0:256] = dot(spread[0], tok_in[...]).astype(BF16)
    projected[:, 256:512] = dot(spread[1], tok_in[...]).astype(BF16)
    reduce_cross(SIG_A)
    reduce_end(CNX_A)
    reduce_end(PIX_A)
    reduce_end(PROJ_A)
    reduce_cross(SIG_B)
    reduce_end(PIX_B)
    reduce_end(SIG_A)
    reduce_end(SIG_B)

    exchange_wait(tok_in, a2b_send, a2b_recv, False)
    for copy in sends:
        copy.wait_send()


def hand_over(*refs):
    for k in range(8):
        refs[8 + k][...] = refs[k][...]


def local(
    sig_in, sig_gain, sig_up, sig_down, cnx_in, cnx_gain, cnx_up, cnx_down,
    pix_in, pix_gain, pix_up, pix_down, proj_weight, owners, cotangent,
):
    any_spec = pl.BlockSpec(memory_space=pl.ANY)
    vmem_spec = pl.BlockSpec(memory_space=pltpu.VMEM)
    vmem = pltpu.VMEM
    dma = pltpu.SemaphoreType.DMA
    widths = [e[0] for e in ENCODERS]
    hiddens = [e[1] for e in ENCODERS]
    scratch = (
        [vmem((4, ROWS, w), BF16) for w in widths]
        + [vmem((4, ROWS, h), BF16) for h in hiddens]
        + [vmem((4 * POOL, h), BF16) for h in hiddens]
        + [vmem((h, w) if f else (w, h), BF16) for w, h, f in zip(widths, hiddens, FLIPPED)]
        + [vmem((h, w), BF16) for w, h in zip(widths, hiddens)]
        + [vmem((4 * POOL, w), BF16) for w in widths]
        + [vmem((6, CHUNKS[n], w), BF16) for n, _, w in UNITS]
        + [vmem((CHUNKS[n], w), BF16) for n, _, w in UNITS]
        + [
            vmem((CAT, LLM), BF16),
            vmem((N_DP * CAP, LLM), BF16),
            vmem((2, N_DP * CAP, SLOTS), BF16),
            vmem((ROWS, ROWS), BF16),
            vmem((2, POOL, SLOTS), BF16),
            vmem((SLOTS, LLM // 2), BF16),
            vmem((SLOTS, LLM // 2), BF16),
            vmem((SLOTS, LLM // 2), BF16),
            vmem((512, LLM), BF16),
            vmem((POOL, CAT), BF16),
            vmem((POOL // 2, CAT), BF16),
            vmem((POOL // 2, CAT), BF16),
            vmem((POOL, CAT), BF16),
            vmem((POOL // 2, CAT), BF16),
            vmem((POOL // 2, CAT), BF16),
            vmem((128, CAT), BF16),
            vmem((3, 4 * PROJ_CHUNK, 128), BF16),
            vmem((8 * PROJ_CHUNK, LLM), BF16),
            vmem((4 * PICK, 384), BF16),
            vmem((8 * PICK, 4 * ROWS), BF16),
        ]
        + [
            dma((11,)),
            dma((N_DP,)), dma((N_DP,)), dma((N_DP,)), dma((N_DP,)),
            dma((4,)), dma((4,)), dma((4,)), dma((4,)), dma((4,)), dma((4,)),
            dma((3, 4)), dma((3, 4)), dma((3, 3)), dma((3, 3)),
            dma((2, 3)), dma((2, 3)),
            dma((3, 4)), dma((3, 4)), dma((3, 4)), dma((3, 4)),
            dma((6, 6)), dma((6, 6)), dma((6,)), dma((6,)),
        ]
    )
    outs = pl.pallas_call(
        kernel,
        out_shape=[
            jax.ShapeDtypeStruct((N_DP * CAP, LLM), BF16),
            *[jax.ShapeDtypeStruct((e[2], e[1]), F32) for e in ENCODERS for _ in range(2)],
            jax.ShapeDtypeStruct((132, LLM), F32),
        ],
        in_specs=[any_spec] * 11 + [vmem_spec] * 4,
        out_specs=[vmem_spec] * 8,
        scratch_shapes=scratch,
        compiler_params=pltpu.CompilerParams(
            collective_id=0, has_side_effects=True, vmem_limit_bytes=64 * 2**20
        ),
        cost_estimate=pl.CostEstimate(flops=2 * 10**10, bytes_accessed=3 * 10**7, transcendentals=0),
    )(
        sig_in, cnx_in, pix_in, sig_up.T, cnx_up, pix_up.T, sig_down, cnx_down, pix_down,
        proj_weight, cotangent, owners.T,
        sig_gain, cnx_gain, pix_gain,
    )
    outs = pl.pallas_call(
        hand_over,
        out_shape=[jax.ShapeDtypeStruct(o.shape, o.dtype) for o in outs],
        in_specs=[vmem_spec] * 8,
        out_specs=[vmem_spec] * 8,
    )(*outs)
    return (outs[0][None], outs[1], outs[2].T, outs[3], outs[4].T, outs[5], outs[6].T, outs[7])


def solution(mesh):
    placed = (
        P("dp", None), P(), P(None, "enc"), P("enc", None),
        P("dp", None), P(), P(None, "enc"), P("enc", None),
        P("dp", None), P(), P(None, "enc"), P("enc", None),
        P(None, "enc"), P("dp", None), P("dp", None, "enc"),
    )
    return jax.shard_map(
        local,
        mesh=mesh,
        in_specs=placed,
        out_specs=(
            P("dp", None, "enc"), P("dp", "enc"), P("enc", "dp"), P("dp", "enc"),
            P("enc", "dp"), P("dp", "enc"), P("enc", "dp"), P("dp", "enc"),
        ),
        check_vma=False,
    )
```

```python
import functools

import jax
import jax.numpy as jnp
from jax import lax
from jax.experimental import pallas as pl
from jax.experimental.pallas import tpu as pltpu
from jax.sharding import PartitionSpec as P

F32 = jnp.float32
BF16 = jnp.bfloat16
MESH = pl.DeviceIdType.MESH
EPSILON = 1e-06
GRID = 64
ROWS = 384
POOL = 96
CAT = 4224
LLM = 512
CAP = 6
PAD = 16
N_DP = 32
SLOTS = N_DP * PAD
PICK = 48
PROJ_CHUNK = 144
TILE = 256

ENCODERS = ((1152, 1076, 36, "z"), (1536, 768, 48, "y"), (1536, 992, 48, "z"))
OFFSETS = (0, 1152, 2688)
PARTS = (40, 48, 48)
CHUNKS = (80, 96, 96, PROJ_CHUNK)
UNITS = ((0, 0, 512), (0, 512, 640), (1, 0, 768), (2, 0, 512), (2, 512, 512), (3, 0, LLM))
SIG_A, SIG_B, CNX_A, PIX_A, PIX_B, PROJ_A = range(6)
FROM = (0, 2, 3, 1)
FLIPPED = (True, False, True)
SIG, CNX, PIX = 0, 1, 2


def dot(left, right):
    return jnp.dot(left, right, preferred_element_type=F32)


def dot_nt(left, right):
    return lax.dot_general(left, right, (((1,), (1,)), ((), ())), preferred_element_type=F32)


def dot_tn(left, right):
    return lax.dot_general(left, right, (((0,), (0,)), ((), ())), preferred_element_type=F32)


def iota(shape, axis):
    return lax.broadcasted_iota(jnp.int32, shape, axis)


def tiles_of(extent, width):
    return [(start, min(width, extent - start)) for start in range(0, extent, width)]


def kernel(*refs):
    ins = refs[0:3]
    ups_hbm = refs[3:6]
    downs_hbm = refs[6:9]
    proj_hbm, cot_hbm, owners, *gains = refs[9:15]
    projected = refs[15]
    grads = ((refs[16], refs[17]), (refs[18], refs[19]), (refs[20], refs[21]), (refs[22],))
    (
        normed_0, normed_1, normed_2, slope_0, slope_1, slope_2, pact_0, pact_1, pact_2,
        up_0, up_1, up_2, down_0, down_1, down_2, gfeat_0, gfeat_1, gfeat_2,
        land_0, land_1, land_2, land_3, land_4, land_5,
        cross_0, cross_1, cross_2, cross_3, cross_4, cross_5,
        proj, cot, spread, perm, place, out_buf, cot_in, tok_in, tok_grads,
        gpart, gpart_sib, gpart_far, bpart, bpart_sib, bpart_far, concat,
        cols_out, cols_in, choose, picked,
        load_sem, a2a_send, a2a_recv, a2b_send, a2b_recv, gt_send, gt_recv, cols_send, cols_recv,
        colf_send, colf_recv, rows_send, rows_recv, sibs_send, sibs_recv, sum_send, sum_recv,
        gf_send, gf_recv, gfs_send, gfs_recv, rs_send, rs_recv, x_send, x_recv,
    ) = refs[23:]
    normed = (normed_0, normed_1, normed_2)
    slope = (slope_0, slope_1, slope_2)
    pact = (pact_0, pact_1, pact_2)
    up = (up_0, up_1, up_2)
    down = (down_0, down_1, down_2)
    gfeat = (gfeat_0, gfeat_1, gfeat_2)
    land = (land_0, land_1, land_2, land_3, land_4, land_5)
    cross = (cross_0, cross_1, cross_2, cross_3, cross_4, cross_5)

    enc = lax.axis_index("enc")
    dp = lax.axis_index("dp")
    core = lax.rem(enc, 2)
    x = lax.div(dp, 16)
    z = lax.rem(lax.div(dp, 4), 4)
    y = lax.rem(dp, 4)
    sibling = {"enc": enc + 1 - 2 * core, "dp": dp}
    far = {"enc": lax.rem(enc + 2, 4), "dp": dp}
    mirror = {"enc": enc, "dp": (1 - x) * 16 + z * 4 + y}
    position = {"z": z, "y": y}

    def step_to(axis, k):
        if axis == "z":
            return {"enc": enc, "dp": x * 16 + lax.rem(z + k, 4) * 4 + y}
        return {"enc": enc, "dp": x * 16 + z * 4 + lax.rem(y + k, 4)}

    sends = []

    def remote(src, dst, send, recv, device):
        return pltpu.make_async_remote_copy(
            src_ref=src, dst_ref=dst, send_sem=send, recv_sem=recv, device_id=device,
            device_id_type=MESH,
        )

    def send(src, dst, send_sem, recv_sem, device):
        copy = remote(src, dst, send_sem, recv_sem, device)
        copy.start()
        sends.append(copy)
        return copy

    barrier = pltpu.get_barrier_semaphore()

    def greet(k, carry):
        other = {"enc": enc, "dp": lax.rem(dp + k, N_DP)}
        pl.semaphore_signal(barrier, inc=1, device_id=other, device_id_type=MESH)
        return carry

    lax.fori_loop(1, N_DP, greet, 0)
    for other in (sibling, far):
        pl.semaphore_signal(barrier, inc=1, device_id=other, device_id_type=MESH)

    loads = {}

    def load(name, src, dst):
        copy = pltpu.make_async_copy(src, dst, load_sem.at[len(loads)])
        copy.start()
        loads[name] = copy

    load("cot", cot_hbm.at[0], cot)
    for i in (CNX, PIX, SIG):
        load(f"in{i}", ins[i], normed[i].at[0])
    load("proj", proj_hbm, proj)
    for i in (CNX, PIX, SIG):
        load(f"up{i}", ups_hbm[i], up[i])
    for i in (CNX, PIX, SIG):
        load(f"down{i}", downs_hbm[i], down[i])

    for q in range(4):
        pooled = iota((POOL, ROWS), 0)
        origin = lax.shift_right_logical(pooled, 5) * 128 + (q // 2) * 64
        origin = origin + lax.bitwise_and(pooled, 31) * 2 + q % 2
        perm[q * POOL:(q + 1) * POOL, :] = (iota((POOL, ROWS), 1) == origin).astype(BF16)

    wide = iota((N_DP * CAP, SLOTS), 1)
    for h in range(2):
        rank = lax.bitwise_and(wide, PAD - 1) - 8 * h
        target = lax.shift_right_logical(wide, 4) * CAP + rank
        hit = (iota((N_DP * CAP, SLOTS), 0) == target) & (rank >= 0) & (rank < CAP)
        spread[h] = hit.astype(BF16)

    diagonal = iota((POOL, POOL), 0) == iota((POOL, POOL), 1)
    owner_ids = jnp.sum(jnp.where(diagonal, owners[...], 0), axis=1, keepdims=True)
    onehot = (owner_ids == iota((POOL, 128), 1)).astype(F32)
    earlier = (iota((POOL, POOL), 1) < iota((POOL, POOL), 0)).astype(BF16)
    before = dot(earlier, onehot.astype(BF16))
    slot_rank = jnp.sum(onehot * before, axis=1, keepdims=True)
    slot = owner_ids.astype(F32) * float(PAD) + slot_rank
    for h in range(2):
        place[h] = (iota((POOL, SLOTS), 1).astype(F32) == slot + 8.0 * h).astype(BF16)

    loads["cot"].wait()
    left = dot_tn(spread[0], cot[:, 0:256]) + dot_tn(spread[1], cot[:, 256:512])
    out_buf[...] = left.astype(BF16)

    def normalize(i):
        width = ENCODERS[i][0]
        own = normed[i].at[0]
        loads[f"in{i}"].wait()
        for start, size in tiles_of(width, 384):
            block = own[:, start:start + size]
            own[:, start:start + size] = dot(perm[...], block).astype(BF16)
        gain = gains[i][...].reshape(1, width)

        def part(k, carry):
            rows = pl.ds(pl.multiple_of(k * 32, 32), 32)
            total = jnp.zeros((32, width), F32)
            for q in range(4):
                cells = pl.ds(pl.multiple_of(q * POOL + k * 32, 32), 32)
                values = own[cells, :].astype(F32)
                total = total + values
                mean = jnp.mean(values, axis=1, keepdims=True)
                centered = values - mean
                var = jnp.mean(centered * centered, axis=1, keepdims=True)
                own[cells, :] = (centered * lax.rsqrt(var + EPSILON) * gain).astype(BF16)
            bpart[rows, OFFSETS[i]:OFFSETS[i] + width] = (total * 0.0625).astype(BF16)
            return carry

        lax.fori_loop(0, POOL // 32, part, 0)

    half = pl.ds(pl.multiple_of(core * 192, 192), 192)
    plane_a = pl.ds(pl.multiple_of(core * 192, 96), POOL)
    plane_b = pl.ds(pl.multiple_of(core * 192 + POOL, 96), POOL)

    def rows_copy(i, k):
        axis = ENCODERS[i][3]
        src = (0, 0, 2, 1)[k]
        dst = (2, 1, 3, 3)[k]
        part = (half, half, plane_a, plane_b)[k]
        device = step_to(axis, 1 if k % 2 == 0 else 3)
        return remote(normed[i].at[src, part], normed[i].at[dst, part],
                      rows_send.at[i, k], rows_recv.at[i, k], device)

    def start(copy):
        copy.start()
        sends.append(copy)

    def sibling_rows(i, k):
        block = normed[i].at[(2, 1, 3)[k], half]
        start(remote(block, block, sibs_send.at[i, k], sibs_recv.at[i, k], sibling))

    def rows_start(i):
        for k in range(2):
            start(rows_copy(i, k))

    def rows_relay(i):
        for k in range(2):
            rows_copy(i, k).wait_recv()
            start(rows_copy(i, 2 + k))
            sibling_rows(i, k)

    def rows_last(i):
        for k in range(2, 4):
            rows_copy(i, k).wait_recv()
        sibling_rows(i, 2)

    other_half = pl.ds(pl.multiple_of((1 - core) * 192, 192), 192)

    def rows_wait(i, k):
        block = normed[i].at[(2, 1, 3)[k], other_half]
        remote(block, block, sibs_send.at[i, k], sibs_recv.at[i, k], sibling).wait_recv()

    def over_tiles(first, last, body):
        whole = last // TILE

        def one(t, carry):
            body(pl.ds(pl.multiple_of(t * TILE, TILE), TILE), TILE)
            return carry

        lax.fori_loop(first // TILE, whole, one, 0)
        if last > whole * TILE:
            body(slice(whole * TILE, last), last - whole * TILE)

    def forward(i, first, count):
        width, hidden, _, _ = ENCODERS[i]

        def tile(cols, size):
            rows = normed[i][first:first + count].reshape(count * ROWS, width)
            if FLIPPED[i]:
                pre = dot_nt(rows, up[i][cols, :])
            else:
                pre = dot(rows, up[i][:, cols])
            cubic = 0.035677408136300125 * (pre * pre)
            linear = cubic + 0.7978845608028654
            tanh = jnp.tanh(pre * linear)
            upper = 0.5 + 0.5 * tanh
            act = pre * upper
            grad = upper + act * (1.0 - tanh) * (linear + (cubic + cubic))
            slope[i][first:first + count, :, cols] = grad.astype(BF16).reshape(count, ROWS, size)
            for s in range(count):
                cell = [act[s * ROWS + q * POOL:s * ROWS + (q + 1) * POOL] for q in range(4)]
                total = (cell[0] + cell[1]) + (cell[2] + cell[3])
                pact[i][(first + s) * POOL:(first + s + 1) * POOL, cols] = total.astype(BF16)

        for start_at, size in tiles_of(hidden, TILE):
            tile(slice(start_at, start_at + size), size)

    def branch(i):
        width = ENCODERS[i][0]
        for start, size in tiles_of(width, 384):
            cols = slice(OFFSETS[i] + start, OFFSETS[i] + start + size)
            value = dot(pact[i][0:POOL, :], down[i][:, start:start + size]) * 0.25
            bpart[:, cols] = (bpart[:, cols].astype(F32) + value).astype(BF16)

    mine = pl.ds(pl.multiple_of(core * 48, 48), 48)
    theirs = pl.ds(pl.multiple_of(48 - core * 48, 48), 48)

    def sum_start(n, part, near):
        send(part.at[theirs], near, sum_send.at[n, 0], sum_recv.at[n, 0], sibling)

    def sum_cross(n, part, near, distant):
        remote(part.at[theirs], near, sum_send.at[n, 0], sum_recv.at[n, 0], sibling).wait_recv()
        part[mine, :] = (part[mine, :].astype(F32) + near[...].astype(F32)).astype(BF16)
        send(part.at[mine], distant, sum_send.at[n, 1], sum_recv.at[n, 1], far)

    def sum_wait(n, part, distant):
        remote(part.at[mine], distant, sum_send.at[n, 1], sum_recv.at[n, 1], far).wait_recv()

    def gfeat_finish(which):
        for i in which:
            width = ENCODERS[i][0]
            cols = slice(OFFSETS[i], OFFSETS[i] + width)
            total = gpart[mine, cols].astype(F32) + gpart_far[:, cols].astype(F32)
            gfeat[i][mine, :] = total.astype(BF16)
            for k in (1, 3, 2):
                start(gfeat_copy(i, k))
            start(gfeat_sibling(i, 0))

    def gfeat_copy(i, k):
        src = gfeat[i].at[mine]
        rows = pl.ds(pl.multiple_of(FROM[k] * POOL + core * 48, 48), 48)
        return remote(src, gfeat[i].at[rows], gf_send.at[i, k], gf_recv.at[i, k],
                      step_to(ENCODERS[i][3], k))

    def gfeat_sibling(i, k, arriving=False):
        at = (48 - core * 48) if arriving else core * 48
        block = gfeat[i].at[pl.ds(pl.multiple_of(FROM[k] * POOL + at, 48), 48)]
        return remote(block, block, gfs_send.at[i, k], gfs_recv.at[i, k], sibling)

    def gfeat_relay(i):
        for k in (1, 3, 2):
            gfeat_copy(i, k).wait_recv()
            start(gfeat_sibling(i, k))

    def gfeat_wait(i):
        for k in range(4):
            gfeat_sibling(i, k, True).wait_recv()

    def concat_finish():
        sum_wait(1, bpart, bpart_far)
        total = bpart[mine, :].astype(F32) + bpart_far[...].astype(F32)
        concat[mine, :] = total.astype(BF16)
        block = concat.at[mine]
        send(block, block, sum_send.at[1, 2], sum_recv.at[1, 2], sibling)

    def concat_wait():
        block = concat.at[theirs]
        remote(block, block, sum_send.at[1, 2], sum_recv.at[1, 2], sibling).wait_recv()

    def exchange(dst, send_sem, recv_sem):
        def one(k, carry):
            other = lax.rem(dp + k, N_DP)
            src = out_buf.at[pl.ds(pl.multiple_of(other * PAD, PAD), PAD)]
            to = dst.at[pl.ds(pl.multiple_of(dp * PAD, PAD), PAD)]
            device = {"enc": enc, "dp": other}
            remote(src, to, send_sem.at[k], recv_sem.at[k], device).start()
            return carry

        lax.fori_loop(1, N_DP, one, 0)
        here = pl.ds(pl.multiple_of(dp * PAD, PAD), PAD)
        dst[here, :] = out_buf[here, :]

    def exchange_wait(dst, send_sem, recv_sem, arrived):
        def one(k, carry):
            other = lax.rem(dp + k, N_DP) if not arrived else lax.rem(dp + N_DP - k, N_DP)
            src = out_buf.at[pl.ds(pl.multiple_of(other * PAD, PAD), PAD)]
            to = dst.at[pl.ds(pl.multiple_of(other * PAD, PAD), PAD)]
            device = {"enc": enc, "dp": other}
            copy = remote(src, to, send_sem.at[k], recv_sem.at[k], device)
            if arrived:
                copy.wait_recv()
            else:
                copy.wait_send()
            return carry

        lax.fori_loop(1, N_DP, one, 0)

    hold = up + (proj,)
    gpicked = perm
    ring = ("y", "z", "y", "z")

    def choice(rows_out, chunks, first):
        lanes_in = 384 if chunks == 0 else 256
        pieces = []
        for b in range(2 if chunks == 0 else chunks):
            r = iota((PICK, lanes_in), 0)
            at = r + first + b * (192 if chunks == 0 else rows_out)
            pieces.append(((iota((PICK, lanes_in), 1) == at) & (r < rows_out)).astype(BF16))
        return jnp.concatenate(pieces, axis=0)

    def backward(i, after):
        width, hidden, rows_out, axis = ENCODERS[i]
        p = position[axis]
        if axis == "y":
            choose[0:2 * PICK, 0:384] = choice(rows_out, 0, p * rows_out)
            for w in range(4):
                rows = slice(w * 2 * PICK, (w + 1) * 2 * PICK)
                cols = slice(w * 384, (w + 1) * 384)
                window = normed[i][:, :, cols].reshape(4 * ROWS, 384)
                picked[rows, :] = dot_nt(choose[0:2 * PICK, 0:384], window).astype(BF16)
                gpicked[rows, :] = dot_nt(choose[0:2 * PICK, 0:384], gfeat[i][:, cols]).astype(BF16)
        else:
            for xx in range(2):
                first = xx * 16 * rows_out + p * 4 * rows_out
                tile = lax.div(first, 128)
                choose[:, 0:256] = choice(rows_out, 4, first - tile * 128)
                rows = slice(xx * 4 * PICK, (xx + 1) * 4 * PICK)
                cols = pl.ds(pl.multiple_of(tile * 128, 128), 256)
                window = normed[i][:, :, cols].reshape(4 * ROWS, 256)
                picked[rows, :] = dot_nt(choose[:, 0:256], window).astype(BF16)
                gpicked[rows, :] = dot_nt(choose[:, 0:256], gfeat[i][:, cols]).astype(BF16)
        def tile(cols, size):
            grad_act = dot_nt(gfeat[i][...], down[i][cols, :])
            for s in range(4):
                grad = grad_act[s * POOL:(s + 1) * POOL].astype(BF16)
                for q in range(4):
                    cells = slice(q * POOL, (q + 1) * POOL)
                    slope[i][s, cells, cols] = slope[i][s, cells, cols] * grad
            upper = dot(picked[...], slope[i][:, :, cols].reshape(4 * ROWS, size))
            lower = dot(gpicked[...], pact[i][:, cols])
            part = PARTS[i]
            for k in range(8):
                at = (k % 2) * 4 * PICK + (k // 2) * PICK
                rows = slice(at, at + part)
                both = jnp.concatenate([upper[rows], lower[rows]], axis=0).astype(BF16)
                hold[i][2 * k * part:2 * (k + 1) * part, cols] = both

        done = 0
        for last in sorted(after):
            over_tiles(done, last, tile)
            done = last
            for action in after[last]:
                action()

    def chunk(n, b, xx):
        size = CHUNKS[n]
        return pl.ds(pl.multiple_of((b * 2 + xx) * size, size), size)

    def lanes_of(u):
        return pl.ds(UNITS[u][1], UNITS[u][2])

    def ring_copy(u, k):
        n = UNITS[u][0]
        axis = ring[n]
        p = position[axis]
        nxt, opp, prv = lax.rem(p + 1, 4), lax.rem(p + 2, 4), lax.rem(p + 3, 4)
        where = ((opp, 0), (opp, 1), (nxt, 1), (prv, 0), (nxt, 0), (prv, 1))[k]
        device = step_to(axis, 1 if k in (0, 2, 4) else 3)
        src = hold[n].at[chunk(n, *where), lanes_of(u)]
        return remote(src, land[u].at[k], rs_send.at[u, k], rs_recv.at[u, k], device)

    def reduce_start(u):
        for k in range(4):
            start(ring_copy(u, k))

    def reduce_mid(u):
        n = UNITS[u][0]
        p = position[ring[n]]
        for k, b, xx in ((0, lax.rem(p + 1, 4), 0), (1, lax.rem(p + 3, 4), 1)):
            ring_copy(u, k).wait_recv()
            rows = chunk(n, b, xx)
            total = hold[n][rows, lanes_of(u)].astype(F32) + land[u][k].astype(F32)
            hold[n][rows, lanes_of(u)] = total.astype(BF16)
            start(ring_copy(u, 4 + k))

    def cross_copy(u):
        n = UNITS[u][0]
        src = hold[n].at[chunk(n, position[ring[n]], 1 - x), lanes_of(u)]
        return remote(src, cross[u], x_send.at[u], x_recv.at[u], mirror)

    def ring_total(u, xx):
        n = UNITS[u][0]
        value = hold[n][chunk(n, position[ring[n]], xx), lanes_of(u)].astype(F32)
        return value + land[u][3 - xx].astype(F32) + land[u][4 + xx].astype(F32)

    def reduce_cross(u):
        n = UNITS[u][0]
        for k in range(2, 6):
            ring_copy(u, k).wait_recv()
        total = ring_total(u, 1 - x).astype(BF16)
        hold[n][chunk(n, position[ring[n]], 1 - x), lanes_of(u)] = total
        start(cross_copy(u))

    def reduce_end(u):
        n, first, _ = UNITS[u]
        cross_copy(u).wait_recv()
        total = ring_total(u, x) + cross[u][...].astype(F32)
        for k, out in enumerate(grads[n]):
            rows, width = out.shape
            last = min(first + UNITS[u][2], width)
            at = k * CHUNKS[n] // 2
            out[:, first:last] = total[at:at + rows, 0:last - first]

    def columns(a):
        def one(j, out):
            k = core * 4 + j
            index = lax.rem(k, 2) * 16 + lax.div(k, 2) * 4 + a
            r = iota((PROJ_CHUNK, 256), 0)
            hit = (iota((PROJ_CHUNK, 256), 1) == r + index * 4) & (r < 132)
            window = concat[:, pl.ds(pl.multiple_of(index * 128, 128), 256)]
            return dot_nt(hit.astype(BF16), window).astype(BF16)

        return one

    col_half = pl.ds(pl.multiple_of(core * 576, 576), 576)
    col_other = pl.ds(pl.multiple_of(576 - core * 576, 576), 576)

    def lane(pos):
        return slice(pos * 128, (pos + 1) * 128)

    def columns_start():
        for k in range(1, 4):
            one = columns(lax.rem(y + k, 4))

            def fill(j, carry, k=k, one=one):
                rows = pl.ds(pl.multiple_of(j * PROJ_CHUNK, PROJ_CHUNK), PROJ_CHUNK)
                cols_out[k - 1, rows, :] = one(j, None)
                return carry

            lax.fori_loop(0, 4, fill, 0)
            send(cols_out.at[k - 1], cols_in.at[col_half, lane(FROM[k])], cols_send.at[k],
                 cols_recv.at[k], step_to("y", k))
        one = columns(y)

        def fill_own(j, carry):
            rows = pl.ds(pl.multiple_of((core * 4 + j) * PROJ_CHUNK, PROJ_CHUNK), PROJ_CHUNK)
            cols_in[rows, lane(0)] = one(j, None)
            return carry

        lax.fori_loop(0, 4, fill_own, 0)
        block = cols_in.at[col_half, lane(0)]
        send(block, block, colf_send.at[0], colf_recv.at[0], sibling)

    def columns_relay():
        for k in range(1, 4):
            block = cols_in.at[col_half, lane(FROM[k])]
            remote(cols_out.at[k - 1], block, cols_send.at[k], cols_recv.at[k],
                   step_to("y", k)).wait_recv()
            send(block, block, colf_send.at[k], colf_recv.at[k], sibling)

    def columns_wait():
        for k in range(4):
            block = cols_in.at[col_other, lane(FROM[k])]
            remote(block, block, colf_send.at[k], colf_recv.at[k], sibling).wait_recv()

    def token_rows(pos):
        return tok_grads.at[pl.ds(pos * 128, 128)]

    def tokens_copy(k):
        return remote(token_rows(0), token_rows(FROM[k]), gt_send.at[k], gt_recv.at[k],
                      step_to("y", k))

    normalize(CNX)
    pl.semaphore_wait(barrier, N_DP + 1)
    exchange(cot_in, a2a_send, a2a_recv)
    rows_start(CNX)
    normalize(PIX)
    rows_start(PIX)
    normalize(SIG)

    loads["proj"].wait()
    exchange_wait(cot_in, a2a_send, a2a_recv, True)
    own_grads = jnp.concatenate(
        [dot(place[0], cot_in[...]), dot(place[1], cot_in[...])], axis=1
    ).astype(BF16)
    tok_grads[0:128, :] = jnp.concatenate([own_grads, jnp.zeros((32, LLM), BF16)], axis=0)
    for k in range(1, 4):
        start(tokens_copy(k))
    for start_at, size in tiles_of(CAT, 384):
        cols = slice(start_at, start_at + size)
        gpart[:, cols] = (dot_nt(tok_grads[0:POOL, :], proj[cols, :]) * 0.25).astype(BF16)
    sum_start(0, gpart, gpart_sib)

    loads[f"up{CNX}"].wait()
    forward(CNX, 0, 1)
    sum_cross(0, gpart, gpart_sib, gpart_far)
    loads[f"up{PIX}"].wait()
    forward(PIX, 0, 1)
    loads[f"up{SIG}"].wait()
    forward(SIG, 0, 1)
    for i in (CNX, PIX, SIG):
        loads[f"down{i}"].wait()
        branch(i)
    sum_start(1, bpart, bpart_sib)
    sum_cross(1, bpart, bpart_sib, bpart_far)
    rows_relay(CNX)
    rows_relay(PIX)
    sum_wait(0, gpart, gpart_far)
    gfeat_finish((CNX, PIX))
    concat[POOL:128, :] = jnp.zeros((32, CAT), BF16)

    rows_wait(CNX, 0)
    rows_wait(CNX, 1)
    forward(CNX, 1, 2)
    rows_wait(PIX, 0)
    rows_wait(PIX, 1)
    rows_last(CNX)
    forward(PIX, 1, 2)
    rows_start(SIG)
    rows_wait(CNX, 2)
    forward(CNX, 3, 1)
    concat_finish()
    gfeat_finish((SIG,))
    concat_wait()

    exchange_wait(cot_in, a2a_send, a2a_recv, False)
    tokens = jnp.zeros((POOL, LLM), F32)
    for start_at, size in tiles_of(CAT, 384):
        cols = slice(start_at, start_at + size)
        tokens = tokens + dot(concat[0:POOL, cols], proj[cols, :])
    tokens = tokens.astype(BF16)
    left = dot_tn(place[0], tokens[:, 0:256]) + dot_tn(place[1], tokens[:, 256:512])
    out_buf[...] = left.astype(BF16)
    exchange(tok_in, a2b_send, a2b_recv)
    columns_start()
    gfeat_relay(CNX)
    rows_last(PIX)

    def do(action, *args):
        return functools.partial(action, *args)

    gfeat_wait(CNX)
    backward(CNX, {768: (do(reduce_start, CNX_A),)})
    gfeat_relay(PIX)
    rows_wait(PIX, 2)
    forward(PIX, 3, 1)
    columns_relay()
    gfeat_wait(PIX)
    backward(PIX, {
        512: (do(reduce_start, PIX_A), do(rows_relay, SIG), do(reduce_mid, CNX_A)),
        992: (do(reduce_start, PIX_B),),
    })
    for k in range(1, 4):
        tokens_copy(k).wait_recv()
    columns_wait()
    for k in range(8):
        rows = slice(k * PROJ_CHUNK, (k + 1) * PROJ_CHUNK)
        proj[rows, :] = dot(cols_in[rows, :], tok_grads[...]).astype(BF16)
    reduce_start(PROJ_A)
    reduce_mid(PIX_A)
    gfeat_relay(SIG)
    rows_wait(SIG, 0)
    rows_wait(SIG, 1)
    forward(SIG, 1, 2)
    rows_last(SIG)
    reduce_mid(PIX_B)
    rows_wait(SIG, 2)
    forward(SIG, 3, 1)
    reduce_mid(PROJ_A)
    gfeat_wait(SIG)
    backward(SIG, {
        512: (do(reduce_start, SIG_A), do(reduce_cross, CNX_A)),
        1076: (do(reduce_start, SIG_B),),
    })
    reduce_mid(SIG_A)
    reduce_cross(PIX_A)
    reduce_cross(PROJ_A)
    reduce_cross(PIX_B)
    reduce_mid(SIG_B)
    exchange_wait(tok_in, a2b_send, a2b_recv, True)
    projected[:, 0:256] = dot(spread[0], tok_in[...]).astype(BF16)
    projected[:, 256:512] = dot(spread[1], tok_in[...]).astype(BF16)
    reduce_cross(SIG_A)
    reduce_end(CNX_A)
    reduce_end(PIX_A)
    reduce_end(PROJ_A)
    reduce_cross(SIG_B)
    reduce_end(PIX_B)
    reduce_end(SIG_A)
    reduce_end(SIG_B)

    exchange_wait(tok_in, a2b_send, a2b_recv, False)
    for copy in sends:
        copy.wait_send()


def hand_over(*refs):
    for k in range(8):
        refs[8 + k][...] = refs[k][...]


def local(
    sig_in, sig_gain, sig_up, sig_down, cnx_in, cnx_gain, cnx_up, cnx_down,
    pix_in, pix_gain, pix_up, pix_down, proj_weight, owners, cotangent,
):
    any_spec = pl.BlockSpec(memory_space=pl.ANY)
    vmem_spec = pl.BlockSpec(memory_space=pltpu.VMEM)
    vmem = pltpu.VMEM
    dma = pltpu.SemaphoreType.DMA
    widths = [e[0] for e in ENCODERS]
    hiddens = [e[1] for e in ENCODERS]
    scratch = (
        [vmem((4, ROWS, w), BF16) for w in widths]
        + [vmem((4, ROWS, h), BF16) for h in hiddens]
        + [vmem((4 * POOL, h), BF16) for h in hiddens]
        + [vmem((h, w) if f else (w, h), BF16) for w, h, f in zip(widths, hiddens, FLIPPED)]
        + [vmem((h, w), BF16) for w, h in zip(widths, hiddens)]
        + [vmem((4 * POOL, w), BF16) for w in widths]
        + [vmem((6, CHUNKS[n], w), BF16) for n, _, w in UNITS]
        + [vmem((CHUNKS[n], w), BF16) for n, _, w in UNITS]
        + [
            vmem((CAT, LLM), BF16),
            vmem((N_DP * CAP, LLM), BF16),
            vmem((2, N_DP * CAP, SLOTS), BF16),
            vmem((ROWS, ROWS), BF16),
            vmem((2, POOL, SLOTS), BF16),
            vmem((SLOTS, LLM // 2), BF16),
            vmem((SLOTS, LLM // 2), BF16),
            vmem((SLOTS, LLM // 2), BF16),
            vmem((512, LLM), BF16),
            vmem((POOL, CAT), BF16),
            vmem((POOL // 2, CAT), BF16),
            vmem((POOL // 2, CAT), BF16),
            vmem((POOL, CAT), BF16),
            vmem((POOL // 2, CAT), BF16),
            vmem((POOL // 2, CAT), BF16),
            vmem((128, CAT), BF16),
            vmem((3, 4 * PROJ_CHUNK, 128), BF16),
            vmem((8 * PROJ_CHUNK, LLM), BF16),
            vmem((4 * PICK, 384), BF16),
            vmem((8 * PICK, 4 * ROWS), BF16),
        ]
        + [
            dma((11,)),
            dma((N_DP,)), dma((N_DP,)), dma((N_DP,)), dma((N_DP,)),
            dma((4,)), dma((4,)), dma((4,)), dma((4,)), dma((4,)), dma((4,)),
            dma((3, 4)), dma((3, 4)), dma((3, 3)), dma((3, 3)),
            dma((2, 3)), dma((2, 3)),
            dma((3, 4)), dma((3, 4)), dma((3, 4)), dma((3, 4)),
            dma((6, 6)), dma((6, 6)), dma((6,)), dma((6,)),
        ]
    )
    outs = pl.pallas_call(
        kernel,
        out_shape=[
            jax.ShapeDtypeStruct((N_DP * CAP, LLM), BF16),
            *[jax.ShapeDtypeStruct((e[2], e[1]), F32) for e in ENCODERS for _ in range(2)],
            jax.ShapeDtypeStruct((132, LLM), F32),
        ],
        in_specs=[any_spec] * 11 + [vmem_spec] * 4,
        out_specs=[vmem_spec] * 8,
        scratch_shapes=scratch,
        compiler_params=pltpu.CompilerParams(
            collective_id=0, has_side_effects=True, vmem_limit_bytes=64 * 2**20
        ),
        cost_estimate=pl.CostEstimate(flops=2 * 10**10, bytes_accessed=3 * 10**7, transcendentals=0),
    )(
        sig_in, cnx_in, pix_in, sig_up.T, cnx_up, pix_up.T, sig_down, cnx_down, pix_down,
        proj_weight, cotangent, owners.T,
        sig_gain, cnx_gain, pix_gain,
    )
    outs = pl.pallas_call(
        hand_over,
        out_shape=[jax.ShapeDtypeStruct(o.shape, o.dtype) for o in outs],
        in_specs=[vmem_spec] * 8,
        out_specs=[vmem_spec] * 8,
    )(*outs)
    return (outs[0][None], outs[1], outs[2].T, outs[3], outs[4].T, outs[5], outs[6].T, outs[7])


def solution(mesh):
    placed = (
        P("dp", None), P(), P(None, "enc"), P("enc", None),
        P("dp", None), P(), P(None, "enc"), P("enc", None),
        P("dp", None), P(), P(None, "enc"), P("enc", None),
        P(None, "enc"), P("dp", None), P("dp", None, "enc"),
    )
    return jax.shard_map(
        local,
        mesh=mesh,
        in_specs=placed,
        out_specs=(
            P("dp", None, "enc"), P("dp", "enc"), P("enc", "dp"), P("dp", "enc"),
            P("enc", "dp"), P("dp", "enc"), P("enc", "dp"), P("dp", "enc"),
        ),
        check_vma=False,
    )
```
